32 devices in a mesh: seq: 8 (over z, y), exp: 4 (over x, core).
Axes of the slice: x: 2, y: 2, z: 4, core: 2. Of those that a mesh axis runs over, the one named last changes fastest.
Arguments:
- tokens: bfloat16 [16384, 1536], P('seq'), may hold values from -6 to 6
- segment_ids: int32 [16384], replicated, may hold values from 0 to 4, as said below
- routes: int32 [16384, 6], P(('seq', 'exp')), may hold values from 0 to 63, all different within a row; in each aligned block of 512 rows (0 to 511, 512 to 1023, ...) at most 96 rows name the same one
- gate_weights: float32 [16384, 6], P(('seq', 'exp')), may hold values from 0.08 to 0.3
- cotangent: bfloat16 [16384, 1536], P(('seq', 'exp')), may hold values from -6 to 6
- norm_in: float32 [1536], replicated, may hold values from 0.5 to 1.5
- proj_z: bfloat16 [1536, 3072], P('seq', 'exp'), may hold values from -0.15625 to 0.15625
- proj_x: bfloat16 [1536, 3072], P('seq', 'exp'), may hold values from -0.15625 to 0.15625
- proj_bc: bfloat16 [1536, 256], replicated, may hold values from -0.15625 to 0.15625
- proj_dt: bfloat16 [1536, 48], P('seq', 'exp'), may hold values from -0.078125 to 0.078125
- conv_weight: float32 [4, 3328], replicated, may hold values from -3 to 3
- conv_bias: float32 [3328], replicated, may hold values from -0.5 to 0.5
- dt_bias: float32 [48], replicated, may hold values from -10 to -3
- decay_log: float32 [48], replicated, may hold values from -1 to 1
- skip_gain: float32 [48], replicated, may hold values from 0.5 to 1.5
- gated_gain: float32 [3072], replicated, may hold values from 0.5 to 1.5
- proj_out: bfloat16 [3072, 1536], P('exp', 'seq'), may hold values from -0.109375 to 0.109375
- norm_mid: float32 [1536], replicated, may hold values from 0.5 to 1.5
- expert_gate: bfloat16 [64, 1536, 512], P('exp', 'seq'), may hold values from -0.15625 to 0.15625
- expert_up: bfloat16 [64, 1536, 512], P('exp', 'seq'), may hold values from -0.15625 to 0.15625
- expert_down: bfloat16 [64, 512, 1536], P('exp', None, 'seq'), may hold values from -1 to 1
- shared_gate: bfloat16 [1536, 1024], replicated, may hold values from -0.15625 to 0.15625
- shared_up: bfloat16 [1536, 1024], replicated, may hold values from -0.15625 to 0.15625
- shared_down: bfloat16 [1024, 1536], replicated, may hold values from -0.375 to 0.375
Outputs:
- block_output: bfloat16 [16384, 1536], P(('seq', 'exp'))
- tokens_grad: float32 [16384, 1536], P(('seq', 'exp'))
- grad_norm_in: float32 [1536], replicated
- grad_proj_z: float32 [1536, 3072], P('seq', 'exp')
- grad_proj_x: float32 [1536, 3072], P('seq', 'exp')
- grad_proj_bc: float32 [1536, 256], replicated
- grad_proj_dt: float32 [1536, 48], P('seq', 'exp')
- grad_conv_weight: float32 [4, 3328], replicated
- grad_conv_bias: float32 [3328], replicated
- grad_dt_bias: float32 [48], replicated
- grad_decay_log: float32 [48], replicated
- grad_skip_gain: float32 [48], replicated
- grad_gated_gain: float32 [3072], replicated
- grad_proj_out: float32 [3072, 1536], P('exp', 'seq')
- grad_norm_mid: float32 [1536], replicated
- grad_expert_gate: float32 [64, 1536, 512], P('exp', 'seq')
- grad_expert_up: float32 [64, 1536, 512], P('exp', 'seq')
- grad_expert_down: float32 [64, 512, 1536], P('exp', None, 'seq')
- grad_shared_gate: float32 [1536, 1024], replicated
- grad_shared_up: float32 [1536, 1024], replicated
- grad_shared_down: float32 [1024, 1536], replicated
The draws below stay inside these ranges and needn't reach their ends.
Inputs may be any that keep to these rules, and one draw needn't show every extreme that they name: `segment_ids`: segment ids never fall along the tokens; tokens with one id form one document. `routes`: in each aligned block of 512 tokens no expert is named by more than 96 assignments.
All inputs are finite; a program needn't handle non-finite values.
Results may differ from the reference program's by a relative error of at most 0.017.
Values may be sent and summed in bfloat16 or wider, within the bound.
No kernel may reach another device: no remote copies, remote signals or barrier semaphores. Data moves between devices by JAX's collectives and lax.ppermute only.
A program may use at most 512 MiB of HBM per device.

```python
import math
from functools import partial
import jax
import jax.numpy as jnp
import numpy as np
from jax import lax

D = 1536
HEADS = 48
HEAD = 64
STATE = 128
CONV = 4
SPAN = 256
EXPERTS = 64
TOP = 6
EXPERT_FF = 512
SHARED_FF = 1024
TOK_SEQ = 2048
INNER = 3072
TOK_EXP = 512
TOKENS = 16384
CAP = 96
N_SEQ = 8
N_EXP = 4


def draw_segment_ids(key, part):
    key = jax.random.fold_in(key, 7)
    head_key, tail_key = jax.random.split(key, 2)
    shard_count = TOKENS // TOK_SEQ
    head_cuts = jax.random.randint(head_key, (2,), TOK_SEQ // 4, 3 * TOK_SEQ // 4, dtype=jnp.int32)
    tail_cuts = (shard_count - 1) * TOK_SEQ + jax.random.randint(tail_key, (2,), TOK_SEQ // 4, 3 * TOK_SEQ // 4, dtype=jnp.int32)
    cut_points = jnp.concatenate([head_cuts, tail_cuts]).astype(jnp.int32)
    positions = jnp.arange(TOKENS, dtype=jnp.int32)
    return jnp.sum((positions[:, None] >= cut_points[None, :]).astype(jnp.int32), axis=1).astype(jnp.int32)


def block_levels(rng, shape, cuts, smallest, top_value):
    level, own = 1.0, jax.random.fold_in(rng, 6)
    for dim, blocks in cuts:
        heights = jnp.exp(jax.random.uniform(jax.random.fold_in(own, dim), (blocks,), jnp.float32, smallest / len(cuts), top_value / len(cuts)))
        level = level * jnp.repeat(heights, shape[dim] // blocks).reshape([-1 if axis == dim else 1 for axis in range(len(shape))])
    return level


def assign_block(own_key, own, number, rows, number_of, top, most, skew):
    sequence = jax.random.permutation(own_key, number_of)
    crowded, common = load_shares(number_of, rows * top, most, skew, True), load_shares(number_of, rows * top, most, skew, False)
    places = jnp.arange(number_of)

    def named(tallies, turn):
        used = int((tallies > 0).sum())
        fixed = max(1, used // 4)
        moved = fixed + (places - fixed + turn * (used - fixed)) % max(1, number_of - fixed)
        return jnp.zeros((number_of,), jnp.int32).at[sequence[jnp.where(places < fixed, places, moved)]].set(jnp.asarray(tallies, jnp.int32))

    tallies = jnp.where(number % 4 == 0, named(crowded, number // 4), named(common, number - number // 4 - 1))
    mixed = jax.random.permutation(jax.random.fold_in(own, 3), number_of)
    source_of, receiver = mixed[0:number_of // 2 * 2:2], mixed[1:number_of // 2 * 2:2]
    room = jnp.minimum(tallies[source_of] - 1, most - tallies[receiver]) // 2
    room = jnp.where((source_of == sequence[0]) | (receiver == sequence[0]) | (tallies[receiver] == 0), 0, jnp.maximum(room, 0))
    moved = jax.random.randint(jax.random.fold_in(own, 4), (number_of // 2,), 0, 1 << 20) % (room + 1)
    tallies = tallies.at[source_of].add(-moved).at[receiver].add(moved)
    labels = jnp.searchsorted(jnp.cumsum(tallies), jnp.arange(rows * top), side="right").astype(jnp.int32)
    grid = labels.reshape(top, rows).T
    grid = grid[jax.random.permutation(jax.random.fold_in(own, 1), rows)]
    turn = jax.random.randint(jax.random.fold_in(own, 2), (rows, 1), 0, top)
    return jnp.take_along_axis(grid, (jnp.arange(top)[None, :] + turn) % top, axis=1)


def load_shares(count, total, reach, slope, full):
    portions = [(1 << 20) // math.isqrt(grade ** slope) + 1 for grade in range(1, count + 1)]
    largest = reach if full else min(reach, max(-(-total // count), total * portions[0] // sum(portions)))
    least = 1 if total - largest >= count - 1 else 0
    holding, spare = [largest] + [least] * (count - 1), total - largest - least * (count - 1)
    while spare > 0:
        candidates = [i for i in range(1, count) if holding[i] < largest] or [i for i in range(1, count) if holding[i] < reach]
        whole, remaining = sum([portions[i] for i in candidates]), spare
        for i in candidates:
            extra = min(reach - holding[i], max(1, remaining * portions[i] // whole), spare)
            holding[i] = holding[i] + extra
            spare = spare - extra
    return np.array(holding)


def gaussian(key, extent, scale, limit, shards=(), held_as=jnp.bfloat16):
    values = jax.random.normal(key, extent, jnp.float32) * scale
    if len(shards) > 0:
        values = block_levels(key, extent, shards, -0.22, 0.18) * values
    return jnp.clip(values, min=-limit, max=limit).astype(held_as)


def setup_inputs(seed: int = 0) -> dict:
    seeds = jax.random.split(jax.random.key(seed), 25)
    tokens = gaussian(seeds[0], (TOKENS, D), 1.0, 6.0, ((0, 8),))
    segment_ids = draw_segment_ids(jax.random.fold_in(seeds[24], 71), 0)
    routes_keys = jax.random.split(jax.random.fold_in(seeds[2], 1), TOKENS // TOK_EXP)
    routes_turns = jax.random.permutation(jax.random.fold_in(seeds[2], 3), TOKENS // TOK_EXP)
    routes = jax.vmap(lambda own, number: assign_block(jax.random.fold_in(seeds[2], 2), own, number, TOK_EXP, EXPERTS, TOP, CAP, 1))(routes_keys, routes_turns).reshape((TOKENS, TOP))
    gate_weights = jnp.clip(jnp.exp(math.log(0.3) - 1.3217559 * jax.random.uniform(seeds[3], (TOKENS, TOP), jnp.float32) ** block_levels(seeds[3], (TOKENS, TOP), ((0, 32),), -0.2, 0.2)), 0.08, 0.3)
    cotangent = gaussian(seeds[4], (TOKENS, D), 1.0, 6.0, ((0, 32),))
    norm_in = jnp.clip(1.0 + 0.1 * jax.random.normal(seeds[5], (D,), jnp.float32), 0.5, 1.5)
    proj_z = gaussian(seeds[6], (D, INNER), D ** -0.5, 0.15625, ((0, 8), (1, 4)))
    proj_x = gaussian(seeds[7], (D, INNER), D ** -0.5, 0.15625, ((0, 8), (1, 4)))
    proj_bc = gaussian(seeds[8], (D, 2 * STATE), D ** -0.5, 0.15625)
    proj_dt = gaussian(seeds[9], (D, HEADS), (4 * D) ** -0.5, 0.078125, ((0, 8), (1, 4)))
    conv_weight = gaussian(seeds[10], (CONV, INNER + 2 * STATE), CONV ** -0.5, 3.0, (), jnp.float32)
    conv_bias = jnp.clip(jax.random.uniform(seeds[11], (INNER + 2 * STATE,), jnp.float32, -0.5, 0.5), -0.5, 0.5)
    dt_bias = jnp.clip(jax.random.uniform(seeds[12], (HEADS,), jnp.float32, -10.0, -3.0), -10.0, -3.0)
    decay_log = jnp.clip(jax.random.uniform(seeds[13], (HEADS,), jnp.float32, -1.0, 1.0), -1.0, 1.0)
    skip_gain = jnp.clip(1.0 + 0.1 * jax.random.normal(seeds[14], (HEADS,), jnp.float32), 0.5, 1.5)
    gated_gain = jnp.clip(1.0 + 0.1 * jax.random.normal(seeds[15], (INNER,), jnp.float32), 0.5, 1.5)
    proj_out = gaussian(seeds[16], (INNER, D), INNER ** -0.5, 0.109375, ((0, 4), (1, 8)))
    norm_mid = jnp.clip(1.0 + 0.1 * jax.random.normal(seeds[17], (D,), jnp.float32), 0.5, 1.5)
    expert_gate = gaussian(seeds[18], (EXPERTS, D, EXPERT_FF), D ** -0.5, 0.15625, ((0, 4), (1, 8)))
    expert_up = gaussian(seeds[19], (EXPERTS, D, EXPERT_FF), D ** -0.5, 0.15625, ((0, 4), (1, 8)))
    expert_down = gaussian(seeds[20], (EXPERTS, EXPERT_FF, D), (EXPERT_FF // 16) ** -0.5, 1.0, ((0, 4), (2, 8)))
    shared_gate = gaussian(seeds[21], (D, SHARED_FF), D ** -0.5, 0.15625)
    shared_up = gaussian(seeds[22], (D, SHARED_FF), D ** -0.5, 0.15625)
    shared_down = gaussian(seeds[23], (SHARED_FF, D), (SHARED_FF // 4) ** -0.5, 0.375)
    return dict(tokens=tokens, segment_ids=segment_ids, routes=routes, gate_weights=gate_weights, cotangent=cotangent, norm_in=norm_in, proj_z=proj_z, proj_x=proj_x, proj_bc=proj_bc, proj_dt=proj_dt, conv_weight=conv_weight, conv_bias=conv_bias, dt_bias=dt_bias, decay_log=decay_log, skip_gain=skip_gain, gated_gain=gated_gain, proj_out=proj_out, norm_mid=norm_mid, expert_gate=expert_gate, expert_up=expert_up, expert_down=expert_down, shared_gate=shared_gate, shared_up=shared_up, shared_down=shared_down)


EPS = 1e-05
HIGH = lax.Precision.HIGHEST
FLOOR = -1e+30

@jax.custom_vjp
def low(v):
    return lax.optimization_barrier(v.astype(jnp.bfloat16)).astype(jnp.float32)

@jax.custom_vjp
def low_back(v):
    return v

def low_keep(v):
    return (low(v), None)

def low_pass(kept, grad):
    return (grad,)

def back_keep(v):
    return (v, None)

def back_low(kept, grad):
    return (low(grad),)
low.defvjp(low_keep, low_pass)
low_back.defvjp(back_keep, back_low)

def matmul(left, right):
    return jnp.dot(left, right, precision=HIGH, preferred_element_type=jnp.float32)

def rms_norm(values, gain):
    return values * lax.rsqrt(lax.optimization_barrier(jnp.mean(values * values, axis=-1, keepdims=True)) + EPS) * gain[None, :]

def same_mask(segs_ext, length):
    return jnp.stack([(segs_ext[tap_index:tap_index + length] == segs_ext[CONV - 1:CONV - 1 + length]).astype(jnp.float32) for tap_index in range(CONV)], axis=1)

def conv_apply(source_ext, kernel, offset, same_seg):
    length = same_seg.shape[0]
    total = jnp.zeros((length, kernel.shape[1]), jnp.float32) + offset[None, :]
    for tap_index in range(kernel.shape[0]):
        total = total + source_ext[tap_index:tap_index + length] * kernel[tap_index][None, :] * same_seg[:, tap_index:tap_index + 1]
    return total

def span_step(decay_rates, carry_state, span_data):
    inputs, b_matrix, c_matrix, step_sizes, segs, seg_prev = span_data
    cum_log = jnp.cumsum(step_sizes * decay_rates[None, :], axis=0)
    positions = jnp.arange(inputs.shape[0], dtype=jnp.int32)
    keep_mask = (segs[:, None] == segs[None, :]) & (positions[:, None] >= positions[None, :])
    spread = cum_log.T[:, :, None] - cum_log.T[:, None, :]
    decay_term = jnp.exp(jnp.where(keep_mask[None], spread, FLOOR))
    scores = matmul(c_matrix, b_matrix.T)
    weights = decay_term * scores[None] * step_sizes.T[:, None, :]
    intra_out = jnp.einsum('hts,shp->thp', weights, inputs, precision=HIGH)
    entry_decay = jnp.exp(cum_log) * (segs == seg_prev).astype(jnp.float32)[:, None]
    carried = jnp.einsum('tn,hpn->thp', c_matrix, carry_state, precision=HIGH) * entry_decay[:, :, None]
    last_seg = segs[-1]
    tail_weight = jnp.exp(cum_log[-1][None, :] - cum_log) * (segs == last_seg).astype(jnp.float32)[:, None] * step_sizes
    kept_decay = jnp.exp(cum_log[-1]) * (last_seg == seg_prev).astype(jnp.float32)
    new_state = carry_state * kept_decay[:, None, None] + jnp.einsum('sh,shp,sn->hpn', tail_weight, inputs, b_matrix, precision=HIGH)
    return (new_state, intra_out + carried)

def ssd_spans(inputs, b_matrix, c_matrix, step_sizes, decay_rates, segs, seg_prev, carry_state):
    length, head_count, head_dim = inputs.shape
    span_count = length // SPAN
    span_prev = jnp.concatenate([jnp.reshape(seg_prev, (1,)).astype(jnp.int32), segs[SPAN - 1:length - 1:SPAN].astype(jnp.int32)])
    span_data = (inputs.reshape(span_count, SPAN, head_count, head_dim), b_matrix.reshape(span_count, SPAN, -1), c_matrix.reshape(span_count, SPAN, -1), step_sizes.reshape(span_count, SPAN, head_count), segs.reshape(span_count, SPAN), span_prev)
    final_state, outputs = lax.scan(jax.checkpoint(partial(span_step, decay_rates)), carry_state, span_data)
    return (outputs.reshape(length, head_count, head_dim), final_state)

def slot_table(routes):
    block_count = N_SEQ * N_EXP
    flat_routes = routes.reshape(block_count, TOK_EXP * TOP).astype(jnp.int32)
    onehot = (flat_routes[:, :, None] == jnp.arange(EXPERTS, dtype=jnp.int32)[None, None, :]).astype(jnp.int32)
    slot_number = lax.optimization_barrier(jnp.sum((jnp.cumsum(onehot, axis=1).astype(jnp.int32) - 1) * onehot, axis=2)).astype(jnp.int32)
    source_block = jnp.arange(block_count, dtype=jnp.int32)[:, None]
    slot_place = (flat_routes * (block_count * CAP) + source_block * CAP + slot_number).astype(jnp.int32)
    token_owner = (jnp.arange(TOKENS * TOP, dtype=jnp.int32) // TOP).astype(jnp.int32)
    slot_owner = jnp.full((EXPERTS * block_count * CAP,), TOKENS, jnp.int32).at[slot_place.reshape(-1)].set(token_owner)
    return (slot_place.reshape(TOKENS, TOP), slot_owner.reshape(EXPERTS, block_count * CAP))

def one_expert(mid_pad, packed):
    gate_w, up_w, down_w, row_index = packed
    taken = low_back(mid_pad[row_index])
    hidden = low(jax.nn.silu(low_back(matmul(taken, gate_w))) * low_back(matmul(taken, up_w)))
    return low_back(low(matmul(hidden, down_w)))

def routed_experts(mid_low, routes, gate_weights, expert_gate, expert_up, expert_down):
    slot_place, slot_owner = slot_table(routes)
    mid_pad = jnp.concatenate([mid_low, jnp.zeros((1, mid_low.shape[1]), jnp.float32)], axis=0)
    outputs = lax.map(jax.checkpoint(partial(one_expert, mid_pad)), (expert_gate, expert_up, expert_down, slot_owner))
    flat_out = outputs.reshape(-1, mid_low.shape[1])
    total = jnp.zeros_like(mid_low)
    for pick_index in range(TOP):
        total = total + gate_weights[:, pick_index:pick_index + 1] * flat_out[slot_place[:, pick_index]]
    return total

def forward(params, tokens_f, segment_ids, routes, gate_weights):
    norm_in, proj_z, proj_x, proj_bc, proj_dt, conv_weight, conv_bias, dt_bias, decay_log, skip_gain, gated_gain, proj_out, norm_mid, expert_gate, expert_up, expert_down, shared_gate, shared_up, shared_down = params
    in_low = low(rms_norm(tokens_f, norm_in))
    gate_z = low_back(matmul(in_low, proj_z))
    raw_x = low_back(matmul(in_low, proj_x))
    raw_bc = matmul(in_low, proj_bc)
    raw_dt = low_back(matmul(in_low, proj_dt))
    source = jnp.concatenate([raw_x, raw_bc], axis=1)
    source_ext = jnp.concatenate([jnp.zeros((CONV - 1, source.shape[1]), jnp.float32), source], axis=0)
    segs_ext = jnp.concatenate([jnp.full((CONV - 1,), -1, jnp.int32), segment_ids.astype(jnp.int32)])
    act = jax.nn.silu(conv_apply(source_ext, conv_weight, conv_bias, same_mask(segs_ext, TOKENS)))
    inputs = low(act[:, :INNER]).reshape(TOKENS, HEADS, HEAD)
    b_matrix = low(act[:, INNER:INNER + STATE])
    c_matrix = low(act[:, INNER + STATE:])
    step_sizes = jax.nn.softplus(raw_dt + dt_bias[None, :])
    decay_rates = -jnp.exp(decay_log)
    scan_y, unused = ssd_spans(inputs, b_matrix, c_matrix, step_sizes, decay_rates, segment_ids.astype(jnp.int32), jnp.int32(-1), jnp.zeros((HEADS, HEAD, STATE), jnp.float32))
    full_y = (scan_y + skip_gain[None, :, None] * inputs).reshape(TOKENS, INNER)
    gated = full_y * jax.nn.silu(gate_z)
    mixer_part = low_back(matmul(low(gated * gated_gain[None, :]), proj_out))
    squares = low_back(lax.optimization_barrier(jnp.sum(gated * gated, axis=1, keepdims=True)))
    scale_mix = lax.rsqrt(squares / INNER + EPS)
    residual = tokens_f + scale_mix * mixer_part
    mid_low = low(rms_norm(residual, norm_mid))
    shared_hid = low(jax.nn.silu(low_back(matmul(mid_low, shared_gate))) * low_back(matmul(mid_low, shared_up)))
    shared_out = matmul(shared_hid, shared_down)
    routed = routed_experts(mid_low, routes, gate_weights, expert_gate, expert_up, expert_down)
    return residual + shared_out + routed

def reference(tokens, segment_ids, routes, gate_weights, cotangent, norm_in, proj_z, proj_x, proj_bc, proj_dt, conv_weight, conv_bias, dt_bias, decay_log, skip_gain, gated_gain, proj_out, norm_mid, expert_gate, expert_up, expert_down, shared_gate, shared_up, shared_down):
    params = (norm_in.astype(jnp.float32), proj_z.astype(jnp.float32), proj_x.astype(jnp.float32), proj_bc.astype(jnp.float32), proj_dt.astype(jnp.float32), conv_weight.astype(jnp.float32), conv_bias.astype(jnp.float32), dt_bias.astype(jnp.float32), decay_log.astype(jnp.float32), skip_gain.astype(jnp.float32), gated_gain.astype(jnp.float32), proj_out.astype(jnp.float32), norm_mid.astype(jnp.float32), expert_gate.astype(jnp.float32), expert_up.astype(jnp.float32), expert_down.astype(jnp.float32), shared_gate.astype(jnp.float32), shared_up.astype(jnp.float32), shared_down.astype(jnp.float32))
    tokens_f = tokens.astype(jnp.float32)

    def run_block(param_set, values):
        return forward(param_set, values, segment_ids, routes, gate_weights.astype(jnp.float32))
    result, pull = jax.vjp(run_block, params, tokens_f)
    param_grads, tokens_grad = pull(cotangent.astype(jnp.float32))
    return (result.astype(jnp.bfloat16), tokens_grad, param_grads[0], param_grads[1], param_grads[2], param_grads[3], param_grads[4], param_grads[5], param_grads[6], param_grads[7], param_grads[8], param_grads[9], param_grads[10], param_grads[11], param_grads[12], param_grads[13], param_grads[14], param_grads[15], param_grads[16], param_grads[17], param_grads[18])
```

```python
from functools import partial

import jax
import jax.numpy as jnp
from jax import lax
from jax.experimental import pallas as pl
from jax.experimental.pallas import tpu as pltpu
from jax.sharding import PartitionSpec as P

CONV = 4
SPAN = 256
LANES = 128
EPS = 1e-05
FLOOR = -1e30
HIGH = lax.Precision.HIGHEST
VMEM_BYTES = 56 * 1024 * 1024
F32 = jnp.float32
BF16 = jnp.bfloat16


def low_dot(left, right):
    return jnp.dot(left, right, preferred_element_type=F32)


def dot_nt(left, right):
    return lax.dot_general(left, right, (((1,), (1,)), ((), ())), preferred_element_type=F32)


def dot_tn(left, right):
    return lax.dot_general(left, right, (((0,), (0,)), ((), ())), preferred_element_type=F32)


def split_dot(values, table):
    high = values.astype(BF16)
    rest = (values - high.astype(F32)).astype(BF16)
    return low_dot(high, table) + low_dot(rest, table)


def exact_sum(triangle, values):
    high = values.astype(BF16)
    rest = values - high.astype(F32)
    middle = rest.astype(BF16)
    small = (rest - middle.astype(F32)).astype(BF16)
    return low_dot(triangle, high) + low_dot(triangle, middle) + low_dot(triangle, small)


def silu_slope(values):
    sigmoid_v = jax.nn.sigmoid(values)
    return sigmoid_v * (1.0 + values * (1.0 - sigmoid_v))


def rms_scale(values):
    return lax.rsqrt(jnp.mean(values * values, axis=-1, keepdims=True) + EPS)


def norm_back(grad_normed, gain, normed, scale):
    weighted = grad_normed * gain[None, :]
    return scale * (weighted - normed * jnp.mean(weighted * normed, axis=-1, keepdims=True))


def compiler_params(steps=1):
    return pltpu.CompilerParams(
        dimension_semantics=("arbitrary",) * steps, vmem_limit_bytes=VMEM_BYTES
    )


def cost(flops, moved, exps=0):
    return pl.CostEstimate(flops=int(flops), bytes_accessed=int(moved), transcendentals=int(exps))


def causal(span):
    rows = lax.broadcasted_iota(jnp.int32, (span, span), 0)
    cols = lax.broadcasted_iota(jnp.int32, (span, span), 1)
    return rows >= cols


def span_terms(steps, marks, seg_row, rates, b_low, c_low):
    span = steps.shape[0]
    keep = causal(span)
    cum = exact_sum(keep.astype(F32).astype(BF16), steps * rates)
    cum_rows = cum.T
    same = marks[:, 6:7] == seg_row
    bias = jnp.where(keep & same, 0.0, FLOOR)
    scores = dot_nt(c_low, b_low)
    last = cum[span - 1 : span, :]
    entry = jnp.exp(cum) * marks[:, 4:5]
    tail = jnp.exp(last - cum) * marks[:, 5:6]
    return cum, cum_rows, bias, scores, last, entry, tail


def scan_forward(
    raw_x,
    raw_s,
    halo,
    marks,
    seg_row,
    taps,
    steps,
    heads,
    spread,
    conv_out,
    x_out,
    bc_out,
    y_out,
    reach_out,
    entries_out,
    last_out,
    ext,
    state,
    total,
):
    turn = pl.program_id(0)
    span, width = raw_x.shape
    channels = taps.shape[1]

    @pl.when(turn == 0)
    def _():
        ext[0:8, :] = halo[...]
        state[...] = jnp.zeros_like(state)
        total[...] = jnp.zeros_like(total)

    @pl.when(turn > 0)
    def _():
        ext[0:8, :] = ext[span : span + 8, :]

    ext[8 : 8 + span, 0:width] = raw_x[...]
    ext[8 : 8 + span, width:channels] = raw_s[:, 0 : channels - width]
    mark = marks[...]
    for start in range(0, channels, LANES):
        cols = slice(start, start + LANES)
        conv = taps[4:5, cols] + taps[3:4, cols] * ext[8 : 8 + span, cols]
        for tap in range(CONV - 1):
            conv = conv + taps[tap : tap + 1, cols] * (
                ext[5 + tap : 5 + tap + span, cols] * mark[:, tap : tap + 1]
            )
        conv_out[:, cols] = conv
        act = (conv * jax.nn.sigmoid(conv)).astype(BF16)
        if start < width:
            x_out[:, cols] = act
        else:
            bc_out[:, start - width : start - width + LANES] = act
    half = (channels - width) // 2
    b_low = bc_out[:, 0:half]
    c_low = bc_out[:, half:]
    step = steps[...]
    rates = heads[1:2, :]
    cum, cum_rows, bias, scores, last, entry, tail = span_terms(
        step, mark, seg_row[0], rates, b_low, c_low
    )
    reach_out[...] = jnp.exp(cum + total[0:1, :]) * mark[:, 3:4]
    total[0:1, :] = total[0:1, :] + last
    table = spread[...]
    entry_wide = split_dot(entry, table)
    xf = x_out[...].astype(F32)
    fed = (xf * split_dot(step, table)).astype(BF16)
    kept = (xf * split_dot(tail * step, table)).astype(BF16)
    entries_out[0] = state[...]
    state_low = state[...].astype(BF16)
    y_out[...] = entry_wide * low_dot(c_low, state_low)
    left_half = lax.broadcasted_iota(jnp.int32, (span, LANES), 1) < LANES // 2
    for pair in range(width // LANES):
        cols = slice(pair * LANES, (pair + 1) * LANES)
        both = []
        for head in (2 * pair, 2 * pair + 1):
            decay = jnp.exp(cum[:, head : head + 1] - cum_rows[head : head + 1, :] + bias)
            both.append(low_dot((decay * scores).astype(BF16), fed[:, cols]))
        y_out[:, cols] = y_out[:, cols] + jnp.where(left_half, both[0], both[1])
    state[...] = state[...] * entry_wide[span - 1 : span, :] + dot_tn(b_low, kept)

    @pl.when(turn == pl.num_programs(0) - 1)
    def _():
        last_out[...] = state[...]


def gate_forward(
    y_local,
    reach,
    bc,
    state_in,
    x,
    gate,
    rows,
    spread,
    weight,
    full_out,
    low_out,
    mixer_out,
    square_out,
):
    half = bc.shape[1] // 2
    c_low = bc[:, half:]
    far = split_dot(reach[...], spread[...]) * low_dot(c_low, state_in[...].astype(BF16))
    full = y_local[...] + far + rows[0:1, :] * x[...].astype(F32)
    full_out[...] = full
    z = gate[...]
    gated = full * (z * jax.nn.sigmoid(z))
    square_out[...] = jnp.sum(gated * gated, axis=1, keepdims=True)
    low = (gated * rows[1:2, :]).astype(BF16)
    low_out[...] = low
    mixer_out[...] = dot_nt(low, weight[...]).astype(BF16)


def gate_backward(
    part_grad,
    square_grad,
    full_y,
    gate,
    x,
    reach,
    bc,
    rows,
    spread,
    weight,
    grad_y_out,
    grad_z_out,
    sums_out,
    direct_out,
):
    turn = pl.program_id(0)
    z = gate[...]
    sig = jax.nn.sigmoid(z)
    act = z * sig
    full = full_y[...]
    gated = full * act
    scaled_grad = low_dot(part_grad[...], weight[...])
    gated_grad = scaled_grad * rows[1:2, :] + 2.0 * gated * square_grad[...]
    grad_full = gated_grad * act
    grad_y_out[...] = grad_full.astype(BF16)
    grad_z_out[...] = (gated_grad * full * (sig * (1.0 + z * (1.0 - sig)))).astype(BF16)
    half = bc.shape[1] // 2
    seen = (grad_full * split_dot(reach[...], spread[...])).astype(BF16)
    direct = dot_tn(bc[:, half:], seen)
    gain_sum = jnp.sum(scaled_grad * gated, axis=0, keepdims=True)
    skip_sum = jnp.sum(grad_full * x[...].astype(F32), axis=0, keepdims=True)

    @pl.when(turn == 0)
    def _():
        sums_out[...] = jnp.zeros_like(sums_out)
        direct_out[...] = jnp.zeros_like(direct_out)

    sums_out[0:1, :] = sums_out[0:1, :] + gain_sum
    sums_out[1:2, :] = sums_out[1:2, :] + skip_sum
    direct_out[...] = direct_out[...] + direct


def scan_backward(
    conv,
    raw_x,
    raw_s,
    raw_x_before,
    raw_s_before,
    halo,
    marks,
    seg_row,
    taps,
    steps,
    heads,
    spread,
    fold,
    x,
    bc,
    full_y,
    grad_y,
    entries,
    passed,
    state_in,
    state_grad,
    rows,
    grad_x_out,
    grad_bc_out,
    grad_step_out,
    tail_out,
    head_out,
    sums_out,
    rates_out,
    ext,
    later0,
    later1,
    later2,
    back,
    turned,
):
    turn = pl.program_id(0)
    span, width = raw_x.shape
    channels = taps.shape[1]
    half = (channels - width) // 2
    later = (later0, later1, later2)

    @pl.when(turn == 0)
    def _():
        back[...] = state_grad[...]
        sums_out[...] = jnp.zeros_like(sums_out)
        rates_out[...] = jnp.zeros_like(rates_out)
        for kept in later:
            kept[span : span + 8, :] = jnp.zeros((8, channels), F32)

    @pl.when(turn > 0)
    def _():
        for kept in later:
            kept[span : span + 8, :] = kept[0:8, :]

    @pl.when(turn == pl.num_programs(0) - 1)
    def _():
        ext[0:8, :] = halo[...]

    @pl.when(turn < pl.num_programs(0) - 1)
    def _():
        ext[0:8, 0:width] = raw_x_before[...]
        ext[0:8, width:channels] = raw_s_before[:, 0 : channels - width]

    ext[8 : 8 + span, 0:width] = raw_x[...]
    ext[8 : 8 + span, width:channels] = raw_s[:, 0 : channels - width]
    mark = marks[...]
    step = steps[...]
    rates = heads[1:2, :]
    b_low = bc[:, 0:half]
    c_low = bc[:, half:]
    cum, cum_rows, bias, scores, last, entry, tail = span_terms(
        step, mark, seg_row[0], rates, b_low, c_low
    )
    table = spread[...]
    entry_wide = split_dot(entry, table)
    tail_wide = split_dot(tail, table)
    step_wide = split_dot(step, table)
    xf = x[...].astype(F32)
    fed_low = (xf * step_wide).astype(BF16)
    fed = fed_low.astype(F32)
    dy_low = grad_y[...]
    dy = dy_low.astype(F32)
    seen = (dy * entry_wide).astype(BF16)
    entered = entries[0] + split_dot(passed[0], table)[0:1, :] * state_in[...]
    entered_low = entered.astype(BF16)
    back_low = back[...].astype(BF16)
    turned_dy = dy.T.astype(BF16)
    left_half = lax.broadcasted_iota(jnp.int32, (span, LANES), 1) < LANES // 2
    score_grad = jnp.zeros((span, span), F32)
    head_rows = LANES // 2
    for pair in range(width // LANES):
        cols = slice(pair * LANES, (pair + 1) * LANES)
        fed_pair = fed_low[:, cols]
        dy_pair = dy[:, cols]
        for side in (0, 1):
            head = 2 * pair + side
            decay = jnp.exp(cum[:, head : head + 1] - cum_rows[head : head + 1, :] + bias)
            weights = (decay * scores).astype(BF16)
            own = jnp.where(left_half if side == 0 else ~left_half, dy_pair, 0.0).astype(BF16)
            score_grad = score_grad + dot_nt(own, fed_pair) * decay
            lanes = slice(head * head_rows, (head + 1) * head_rows)
            turned[lanes, :] = low_dot(turned_dy[lanes, :], weights)
    score_low = score_grad.astype(BF16)
    inner = turned[...].T
    far = tail_wide * low_dot(b_low, back_low)
    fed_grad = inner + far
    skip = rows[0:1, :]
    scan_y = full_y[...] - skip * xf
    summed = fold[...]
    far_sums = split_dot(fed * far, summed)
    kept_row = jnp.sum(back[...] * entered, axis=0, keepdims=True) * entry_wide[span - 1 : span, :]
    kept_sum = split_dot(jnp.broadcast_to(kept_row, (8, width)), summed)[0:1, :]
    log_grad = split_dot(dy * scan_y - fed * fed_grad, summed)
    ends = jnp.sum(far_sums, axis=0, keepdims=True) + kept_sum
    rows_i = lax.broadcasted_iota(jnp.int32, (span, span), 0)
    cols_i = lax.broadcasted_iota(jnp.int32, (span, span), 1)
    upper = (cols_i >= rows_i).astype(F32).astype(BF16)
    rate_step_grad = exact_sum(upper, log_grad) + ends
    grad_step_out[...] = split_dot(fed_grad * xf, summed) + rates * rate_step_grad
    rates_out[0:1, :] = rates_out[0:1, :] + jnp.sum(rate_step_grad * step, axis=0, keepdims=True)
    c_grad = dot_nt(seen, entered_low) + low_dot(score_low, b_low)
    b_grad = dot_nt((fed * tail_wide).astype(BF16), back_low) + dot_tn(score_low, c_low)
    back[...] = back[...] * entry_wide[span - 1 : span, :] + dot_tn(c_low, seen)
    x_grad = fed_grad * step_wide + skip * dy
    for start in range(0, channels, LANES):
        cols = slice(start, start + LANES)
        if start < width:
            active = x_grad[:, cols]
        elif start < width + half:
            active = b_grad
        else:
            active = c_grad
        grad = active * silu_slope(conv[:, cols])

        @pl.when(turn == pl.num_programs(0) - 1)
        def _():
            head_out[:, cols] = grad[0:8, :]

        source = taps[3:4, cols] * grad
        sums_out[4:5, cols] = sums_out[4:5, cols] + jnp.sum(grad, axis=0, keepdims=True)
        sums_out[3:4, cols] = sums_out[3:4, cols] + jnp.sum(
            grad * ext[8 : 8 + span, cols], axis=0, keepdims=True
        )
        for tap in range(CONV - 1):
            masked = grad * mark[:, tap : tap + 1]
            later[tap][0:span, cols] = masked
            sums_out[tap : tap + 1, cols] = sums_out[tap : tap + 1, cols] + jnp.sum(
                masked * ext[5 + tap : 5 + tap + span, cols], axis=0, keepdims=True
            )
            shift = CONV - 1 - tap
            source = source + taps[tap : tap + 1, cols] * later[tap][shift : shift + span, cols]
        if start < width:
            grad_x_out[:, cols] = source.astype(BF16)
        else:
            grad_bc_out[:, start - width : start - width + LANES] = source.astype(BF16)

        @pl.when(turn == 0)
        def _():
            tail_out[:, cols] = source[span - 8 : span, :]


def dispatch_kernel(weighted, *refs):
    if weighted:
        rows, places, gates, out = refs
    else:
        rows, places, out = refs
    experts, _, slots, _ = out.shape
    count = rows.shape[0]
    slot = lax.broadcasted_iota(jnp.int32, (slots, count), 0)
    hits = [slot == places[0, e : e + 1, :] for e in range(experts)]
    chosen = jnp.concatenate([hit.astype(F32).astype(BF16) for hit in hits], axis=0)
    taken = low_dot(chosen, rows[...])
    for e in range(experts):
        part = taken[e * slots : (e + 1) * slots, :]
        if weighted:
            part = part * jnp.sum(
                jnp.where(hits[e], gates[0, e : e + 1, :], 0.0), axis=1, keepdims=True
            )
        out[e, 0] = part.astype(BF16)


def dispatch(rows, places, slots, gates=None):
    blocks, experts, count = places.shape
    width = rows.shape[1]
    arrays = (rows, places) if gates is None else (rows, places, gates)
    small = pl.BlockSpec((1, experts, count), lambda b: (b, 0, 0))
    return pl.pallas_call(
        partial(dispatch_kernel, gates is not None),
        grid=(blocks,),
        in_specs=[pl.BlockSpec((count, width), lambda b: (b, 0))] + [small] * (len(arrays) - 1),
        out_specs=pl.BlockSpec((experts, 1, slots, width), lambda b: (0, b, 0, 0)),
        out_shape=jax.ShapeDtypeStruct((experts, blocks, slots, width), BF16),
        compiler_params=compiler_params(),
        cost_estimate=cost(
            2 * blocks * experts * slots * count * width,
            2 * rows.size + 2 * experts * blocks * slots * width,
        ),
        name="dispatch",
    )(*arrays)


def expert_kernel(pieces, me, got, grad_got, *refs):
    weights = refs[: 3 * pieces]
    hid_out, a_out, b_out, res_out, row_out, gate, up, down = refs[3 * pieces :]
    part = weights[0].shape[1]
    for kind, full in enumerate((gate, up, down)):
        for piece in range(pieces):
            start = pl.multiple_of((me[0] ^ piece) * part, part)
            full[pl.ds(start, part), :] = weights[kind * pieces + piece][0]
    blocks, slots, width = got.shape[1:]
    step = max(1, min(blocks, 384 // slots))
    for first in range(0, blocks, step):
        rows = slice(first * slots, (first + step) * slots)
        taken = got[0, first : first + step].reshape(step * slots, width)
        taken_grad = grad_got[0, first : first + step].reshape(step * slots, width)
        a = low_dot(taken, gate[...])
        b = low_dot(taken, up[...])
        hid_grad = low_dot(taken_grad, down[...])
        sig = jax.nn.sigmoid(a)
        act = a * sig
        hid = (act * b).astype(BF16)
        a_grad = (hid_grad * b * (sig * (1.0 + a * (1.0 - sig)))).astype(BF16)
        b_grad = (hid_grad * act).astype(BF16)
        hid_out[0, rows, :] = hid
        a_out[0, rows, :] = a_grad
        b_out[0, rows, :] = b_grad
        res = dot_nt(hid, down[...]).astype(BF16)
        row = (dot_nt(a_grad, gate[...]) + dot_nt(b_grad, up[...])).astype(BF16)
        res_out[0, first : first + step] = res.reshape(step, slots, width)
        row_out[0, first : first + step] = row.reshape(step, slots, width)


def run_experts(me, got, grad_got, gate, up, down):
    experts, blocks, slots, width = got.shape
    pieces = len(gate)
    part, hidden = gate[0].shape[1:]
    total = blocks * slots
    wide = pl.BlockSpec((1, blocks, slots, width), lambda e, me: (e, 0, 0, 0))
    narrow = pl.BlockSpec((1, total, hidden), lambda e, me: (e, 0, 0))
    piece = pl.BlockSpec((1, part, hidden), lambda e, me: (e, 0, 0))
    hid_shape = jax.ShapeDtypeStruct((experts, total, hidden), BF16)
    row_shape = jax.ShapeDtypeStruct(got.shape, BF16)
    return pl.pallas_call(
        partial(expert_kernel, pieces),
        grid_spec=pltpu.PrefetchScalarGridSpec(
            num_scalar_prefetch=1,
            grid=(experts,),
            in_specs=[wide, wide] + [piece] * (3 * pieces),
            out_specs=[narrow] * 3 + [wide] * 2,
            scratch_shapes=[pltpu.VMEM((width, hidden), BF16)] * 3,
        ),
        out_shape=[hid_shape] * 3 + [row_shape] * 2,
        compiler_params=compiler_params(),
        cost_estimate=cost(
            12 * experts * total * width * hidden,
            8 * got.size + 6 * experts * width * hidden,
            experts * total * hidden,
        ),
        name="experts",
    )(me, got, grad_got, *gate, *up, *down)


def expert_grad_kernel(pieces, me, got, grad_got, hid, a_grad, b_grad, *refs):
    outs, (gate, up, down) = refs[: 3 * pieces], refs[3 * pieces :]
    blocks, slots, width = got.shape[1:]
    part = outs[0].shape[1]
    total = blocks * slots
    step = 256
    for start in range(0, width, step):
        cols = slice(start, start + step)
        taken = got[0, :, :, cols].reshape(total, step)
        taken_grad = grad_got[0, :, :, cols].reshape(total, step)
        gate[cols, :] = dot_tn(taken, a_grad[0]).astype(BF16)
        up[cols, :] = dot_tn(taken, b_grad[0]).astype(BF16)
        down[cols, :] = dot_tn(taken_grad, hid[0]).astype(BF16)
    for kind, full in enumerate((gate, up, down)):
        for piece in range(pieces):
            start = pl.multiple_of((me[0] ^ piece) * part, part)
            outs[kind * pieces + piece][0] = full[pl.ds(start, part), :]


def expert_grads(me, got, grad_got, hid, a_grad, b_grad, pieces):
    experts, blocks, slots, width = got.shape
    total, hidden = hid.shape[1:]
    part = width // pieces
    wide = pl.BlockSpec((1, blocks, slots, width), lambda e, me: (e, 0, 0, 0))
    narrow = pl.BlockSpec((1, total, hidden), lambda e, me: (e, 0, 0))
    piece = pl.BlockSpec((1, part, hidden), lambda e, me: (e, 0, 0))
    outs = pl.pallas_call(
        partial(expert_grad_kernel, pieces),
        grid_spec=pltpu.PrefetchScalarGridSpec(
            num_scalar_prefetch=1,
            grid=(experts,),
            in_specs=[wide] * 2 + [narrow] * 3,
            out_specs=[piece] * (3 * pieces),
            scratch_shapes=[pltpu.VMEM((width, hidden), BF16)] * 3,
        ),
        out_shape=[jax.ShapeDtypeStruct((experts, part, hidden), BF16)] * (3 * pieces),
        compiler_params=compiler_params(),
        cost_estimate=cost(
            6 * experts * total * width * hidden, 4 * got.size + 6 * experts * width * hidden
        ),
        name="expert_grads",
    )(me, got, grad_got, hid, a_grad, b_grad)
    return [outs[kind * pieces : (kind + 1) * pieces] for kind in range(3)]


def combine_kernel(weighted, turned, *refs):
    if weighted:
        rows, places, table, number, gates, hidden, weight, out = refs
    else:
        rows, places, table, number, hidden, weight, out = refs
    experts, _, slots, width = rows.shape
    wide = low_dot(places[0], table[...])
    factor = low_dot(gates[0], table[...]) if weighted else 1.0
    chosen = jnp.where(wide == number[...], factor, 0.0).astype(BF16)
    total = low_dot(chosen, rows[:, 0].reshape(experts * slots, width))
    dense = dot_nt if turned else low_dot
    out[...] = (total + dense(hidden[...], weight[...])).astype(BF16)


def combine(rows, places, hidden, weight, turned, gates=None):
    experts, blocks, slots, width = rows.shape
    count = places.shape[1]
    expert_of = jnp.arange(experts * slots, dtype=jnp.int32) // slots
    table = (jnp.arange(experts, dtype=jnp.int32)[:, None] == expert_of[None, :]).astype(BF16)
    number = (jnp.arange(experts * slots, dtype=jnp.int32) % slots).astype(F32)[None, :]
    small = pl.BlockSpec((1, count, experts), lambda b: (b, 0, 0))
    arrays = [rows, places, table, number]
    specs = [
        pl.BlockSpec((experts, 1, slots, width), lambda b: (0, b, 0, 0)),
        small,
        pl.BlockSpec(table.shape, lambda b: (0, 0)),
        pl.BlockSpec(number.shape, lambda b: (0, 0)),
    ]
    if gates is not None:
        arrays.append(gates)
        specs.append(small)
    arrays += [hidden, weight]
    specs += [
        pl.BlockSpec((count, hidden.shape[1]), lambda b: (b, 0)),
        pl.BlockSpec(weight.shape, lambda b: (0, 0)),
    ]
    return pl.pallas_call(
        partial(combine_kernel, gates is not None, turned),
        grid=(blocks,),
        in_specs=specs,
        out_specs=pl.BlockSpec((count, width), lambda b: (b, 0)),
        out_shape=jax.ShapeDtypeStruct((blocks * count, width), BF16),
        compiler_params=compiler_params(),
        cost_estimate=cost(
            2 * blocks * count * width * (experts * slots + hidden.shape[1]),
            2 * rows.size + 2 * blocks * count * width,
        ),
        name="combine",
    )(*arrays)


def swap(block, axis, stride):
    return lax.ppermute(
        block, axis, [(i, i ^ stride) for i in range(lax.axis_size(axis))]
    )


def bits(count):
    return [1 << i for i in range(count.bit_length() - 1)]


def bit_of(axis, stride):
    return (lax.axis_index(axis) // stride) % 2


def gather_rows(block, axis, strides):
    for stride in strides:
        other = swap(block, axis, stride)
        mine = jnp.concatenate([block, other], axis=0)
        theirs = jnp.concatenate([other, block], axis=0)
        block = jnp.where(bit_of(axis, stride) == 0, mine, theirs)
    return block


def scatter_rows(block, axis, strides):
    for stride in reversed(strides):
        half = block.shape[0] // 2
        place = bit_of(axis, stride)
        kept = lax.dynamic_slice_in_dim(block, place * half, half, 0)
        sent = lax.dynamic_slice_in_dim(block, (1 - place) * half, half, 0)
        block = (kept.astype(F32) + swap(sent, axis, stride).astype(F32)).astype(block.dtype)
    return block


def gather_group(block, steps):
    cols = block.shape[1] // 2
    halves = []
    for part, order in ((block[:, :cols], (0, 1)), (block[:, cols:], (1, 0))):
        known = {0: part}
        numbers = list(order) + list(range(2, len(steps)))
        for number in numbers:
            axis, stride = steps[number]
            got = {place | 1 << number: swap(v, axis, stride) for place, v in known.items()}
            known.update(got)
        halves.append(jnp.concatenate([known[place] for place in range(len(known))], axis=0))
    return jnp.concatenate(halves, axis=1)


def scatter_group(block, steps):
    count = 1 << len(steps)
    rows, width = block.shape[0] // count, block.shape[1]
    cols = width // 2
    halves = []
    for start, order in ((0, (0, 1)), (cols, (1, 0))):
        known = {
            place: lax.slice(block, (place * rows, start), ((place + 1) * rows, start + cols))
            for place in range(count)
        }
        for number in list(reversed(range(2, len(steps)))) + list(reversed(order)):
            axis, stride = steps[number]
            flag = 1 << number
            known = {
                place: (
                    v.astype(F32) + swap(known[place | flag], axis, stride).astype(F32)
                ).astype(BF16 if len(known) > 2 else F32)
                for place, v in known.items()
                if not place & flag
            }
        halves.append(known[0])
    return jnp.concatenate(halves, axis=1)


def spread_weights(shard, low_z, other_strides):
    half = shard.shape[0] // 2
    place = bit_of("seq", low_z)
    kept = lax.dynamic_slice_in_dim(shard, place * half, half, 0)
    sent = lax.dynamic_slice_in_dim(shard, (1 - place) * half, half, 0)
    known = {0: kept, low_z: swap(sent, "seq", low_z)}
    for stride in other_strides:
        known.update({at | stride: swap(v, "seq", stride) for at, v in known.items()})
    return [known[at] for at in range(len(known))]


def collect_weights(pieces, low_z, other_strides):
    known = dict(enumerate(pieces))
    for stride in reversed(other_strides):
        known = {
            at: (v.astype(F32) + swap(known[at | stride], "seq", stride).astype(F32)).astype(BF16)
            for at, v in known.items()
            if not at & stride
        }
    mine, other = known[0], swap(known[low_z], "seq", low_z)
    first = bit_of("seq", low_z) == 0
    return jnp.concatenate(
        [jnp.where(first, mine, other), jnp.where(first, other, mine)], axis=0
    ).astype(F32)


def gather_exp(block, strides):
    known = {0: block}
    for stride in strides:
        known.update({at | stride: swap(v, "exp", stride) for at, v in known.items()})
    for stride in strides:
        flipped = bit_of("exp", stride) == 1
        known = {at: jnp.where(flipped, known[at ^ stride], v) for at, v in known.items()}
    return jnp.concatenate([known[at] for at in range(len(known))], axis=0)


def scatter_exp(blocks, strides):
    place = lax.axis_index("exp")
    known = {
        at: lax.dynamic_index_in_dim(blocks, place ^ at, 0, False) for at in range(blocks.shape[0])
    }
    for stride in reversed(strides):
        known = {
            at: (v.astype(F32) + swap(known[at | stride], "exp", stride).astype(F32)).astype(
                F32 if len(known) == 2 else v.dtype
            )
            for at, v in known.items()
            if not at & stride
        }
    return known[0]


def earlier_states(through, state, strides):
    before = jnp.zeros_like(state)
    whole, decay = state, through
    reach = jnp.ones_like(through)
    for stride in strides:
        other = swap(whole.astype(BF16), "seq", stride).astype(F32)
        other_decay = swap(decay, "seq", stride)
        high = bit_of("seq", stride) == 1
        before = jnp.where(high, before + reach * other, before)
        reach = jnp.where(high, reach * other_decay, reach)
        whole = jnp.where(high, whole + decay * other, other + other_decay * whole)
        decay = decay * other_decay
    return before


def later_grads(through, direct, strides):
    after = jnp.zeros_like(direct)
    whole, decay = direct, through
    reach = jnp.ones_like(through)
    for stride in strides:
        other = swap(whole.astype(BF16), "seq", stride).astype(F32)
        other_decay = swap(decay, "seq", stride)
        low = bit_of("seq", stride) == 0
        after = jnp.where(low, after + reach * other, after)
        reach = jnp.where(low, reach * other_decay, reach)
        whole = jnp.where(low, whole + decay * other, other + other_decay * whole)
        decay = decay * other_decay
    return after


def per_device(
    tokens,
    segment_ids,
    routes,
    gate_weights,
    cotangent,
    norm_in,
    proj_z,
    proj_x,
    proj_bc,
    proj_dt,
    conv_weight,
    conv_bias,
    dt_bias,
    decay_log,
    skip_gain,
    gated_gain,
    proj_out,
    norm_mid,
    expert_gate,
    expert_up,
    expert_down,
    shared_gate,
    shared_up,
    shared_down,
):
    seq_pos = lax.axis_index("seq")
    exp_pos = lax.axis_index("exp")
    exp_count = lax.axis_size("exp")
    seq_count = lax.axis_size("seq")
    length, model_width = tokens.shape
    rows_here, top_count = routes.shape
    inner_width = gated_gain.shape[0]
    head_total = dt_bias.shape[0]
    pair_width = proj_bc.shape[1]
    state_dim = pair_width // 2
    local_width = proj_x.shape[1]
    head_count = proj_dt.shape[1]
    channels = local_width + pair_width
    col_start = exp_pos * local_width
    head_start = exp_pos * head_count
    low_z = seq_count // 4
    seq_strides = bits(seq_count)
    weight_strides = [2 * low_z] + bits(low_z)
    exp_strides = list(reversed(bits(exp_count)))
    steps_group = [("seq", low_z)] + [("exp", stride) for stride in exp_strides]
    span_count = length // SPAN

    pad_dt = jnp.pad(proj_dt, ((0, 0), (0, LANES - head_count)))
    weight_xdt = lax.all_gather(
        jnp.concatenate([proj_x, pad_dt], axis=1), "seq", axis=0, tiled=True
    )
    weight_z = lax.all_gather(proj_z, "seq", axis=0, tiled=True)
    weight_out = lax.all_gather(proj_out.T, "seq", axis=0, tiled=True)
    weight_x, weight_dt = weight_xdt[:, :local_width], weight_xdt[:, local_width:]

    half_experts = expert_gate.shape[0] // 2
    down_pieces = spread_weights(expert_down.transpose(0, 2, 1), low_z, weight_strides)
    gate_pieces = spread_weights(expert_gate, low_z, weight_strides)
    up_pieces = spread_weights(expert_up, low_z, weight_strides)

    def small_group(block):
        known = {0: block}
        for number, (axis, stride) in enumerate(steps_group):
            known.update({at | 1 << number: swap(v, axis, stride) for at, v in known.items()})
        return jnp.concatenate([known[at] for at in range(len(known))], axis=0)

    block_count = 1 << len(steps_group)
    routes_all = small_group(routes).reshape(block_count, rows_here, top_count)
    gates_all = small_group(gate_weights).reshape(block_count, rows_here, top_count)
    cot_all = gather_group(cotangent, steps_group)
    experts_here = expert_gate.shape[0]
    capacity = 2 * rows_here * top_count // (experts_here * exp_count)
    first_expert = exp_pos * experts_here + bit_of("seq", low_z) * half_experts
    expert_ids = first_expert + jnp.arange(half_experts, dtype=jnp.int32)
    named = routes_all[:, :, :, None] == expert_ids
    hit = jnp.any(named, axis=2)
    gate_of = jnp.sum(jnp.where(named, gates_all[:, :, :, None], 0.0), axis=2)
    order = jnp.tril(jnp.ones((rows_here, rows_here), BF16))
    rank = jnp.einsum("ts,bse->bte", order, hit.astype(BF16), preferred_element_type=F32)
    places = jnp.where(hit, rank - 1.0, -1.0)
    place_cols = places.astype(BF16)
    place_rows = places.transpose(0, 2, 1).astype(jnp.int32)
    gate_cols = gate_of.astype(BF16)
    gate_rows = gate_of.transpose(0, 2, 1)
    grad_got = dispatch(cot_all, place_rows, capacity, gate_rows)

    hidden_part = shared_gate.shape[1] // block_count
    group_pos = bit_of("seq", low_z) * exp_count + exp_pos
    hidden_start = group_pos * hidden_part
    shared_in = jnp.concatenate(
        [
            lax.dynamic_slice_in_dim(shared_gate, hidden_start, hidden_part, 1),
            lax.dynamic_slice_in_dim(shared_up, hidden_start, hidden_part, 1),
        ],
        axis=1,
    )
    shared_back = lax.dynamic_slice_in_dim(shared_down, hidden_start, hidden_part, 0)
    grad_shid = dot_nt(cot_all, shared_back)

    tokens_f = tokens.astype(F32)
    scale_in = rms_scale(tokens_f)
    in_low = (tokens_f * scale_in * norm_in[None, :]).astype(BF16)
    raw_x = low_dot(in_low, weight_x)
    raw_s = low_dot(in_low, jnp.concatenate([proj_bc, weight_dt], axis=1))
    gate_z = low_dot(in_low, weight_z)
    last_rows = jnp.concatenate([raw_x[length - 8 :], raw_s[length - 8 :, :pair_width]], axis=1)
    halo = lax.ppermute(last_rows, "seq", [(i, i + 1) for i in range(seq_count - 1)])
    padded_ids = jnp.concatenate([jnp.full((CONV - 1,), -1, jnp.int32), segment_ids])
    segs_ext = lax.dynamic_slice_in_dim(padded_ids, seq_pos * length, length + CONV - 1)
    segs = segs_ext[CONV - 1 :]
    spans = segs.reshape(span_count, SPAN)
    before = jnp.concatenate([segs_ext[CONV - 2 : CONV - 1], spans[:-1, -1]])
    marks = jnp.stack(
        [(segs_ext[tap : tap + length] == segs).astype(F32) for tap in range(CONV - 1)]
        + [
            (segs == segs_ext[CONV - 2]).astype(F32),
            (spans == before[:, None]).astype(F32).reshape(length),
            (spans == spans[:, -1:]).astype(F32).reshape(length),
            segs.astype(F32),
            jnp.zeros((length,), F32),
        ],
        axis=1,
    )
    seg_rows = segs.astype(F32).reshape(span_count, 1, SPAN)

    def local_cols(values):
        mine = lax.dynamic_slice_in_dim(values, col_start, local_width, values.ndim - 1)
        return jnp.concatenate([mine, values[..., inner_width:]], axis=-1)

    taps = jnp.concatenate(
        [
            local_cols(conv_weight),
            local_cols(conv_bias)[None, :],
            jnp.zeros((3, channels), F32),
        ],
        axis=0,
    )
    pad_heads = (0, LANES - head_count)
    dt_local = jnp.pad(lax.dynamic_slice_in_dim(dt_bias, head_start, head_count), pad_heads)
    rates_local = jnp.pad(
        -jnp.exp(lax.dynamic_slice_in_dim(decay_log, head_start, head_count)), pad_heads
    )
    lane_on = jnp.arange(LANES) < head_count
    raw_dt = raw_s[:, pair_width:] + dt_local[None, :]
    step_sizes = jnp.where(lane_on[None, :], jax.nn.softplus(raw_dt), 0.0)
    heads = jnp.concatenate(
        [dt_local[None, :], rates_local[None, :], jnp.zeros((6, LANES), F32)], axis=0
    )
    head_dim = local_width // head_count
    spread_f = (
        jnp.arange(LANES)[:, None] == (jnp.arange(local_width) // head_dim)[None, :]
    ).astype(F32)
    spread = spread_f.astype(BF16)

    def tile(cols, turn=lambda i: i):
        return pl.BlockSpec((SPAN, cols), lambda i: (turn(i), 0))

    def whole(*shape):
        return pl.BlockSpec(shape, lambda i: (0,) * len(shape))

    def seg_tile(turn=lambda i: i):
        return pl.BlockSpec((1, 1, SPAN), lambda i: (turn(i), 0, 0))

    shape = jax.ShapeDtypeStruct
    elements = length * SPAN * head_count
    scan_cost = cost(
        4 * elements * LANES, length * (channels * 8 + local_width * 8 + 4096), elements
    )
    conv_out, inputs, bc_low, local_y, reach, entries, last_state = pl.pallas_call(
        scan_forward,
        grid=(span_count,),
        in_specs=[
            tile(local_width),
            tile(raw_s.shape[1]),
            whole(8, channels),
            tile(8),
            seg_tile(),
            whole(8, channels),
            tile(LANES),
            whole(8, LANES),
            whole(LANES, local_width),
        ],
        out_specs=[
            tile(channels),
            tile(local_width),
            tile(pair_width),
            tile(local_width),
            tile(LANES),
            pl.BlockSpec((1, state_dim, local_width), lambda i: (i, 0, 0)),
            whole(state_dim, local_width),
        ],
        out_shape=[
            shape((length, channels), F32),
            shape((length, local_width), BF16),
            shape((length, pair_width), BF16),
            shape((length, local_width), F32),
            shape((length, LANES), F32),
            shape((span_count, state_dim, local_width), F32),
            shape((state_dim, local_width), F32),
        ],
        scratch_shapes=[
            pltpu.VMEM((SPAN + 8, channels), F32),
            pltpu.VMEM((state_dim, local_width), F32),
            pltpu.VMEM((8, LANES), F32),
        ],
        compiler_params=compiler_params(),
        cost_estimate=scan_cost,
        name="scan_forward",
    )(raw_x, raw_s, halo, marks, seg_rows, taps, step_sizes, heads, spread)

    through = jnp.dot(reach[length - 1 :], spread_f, precision=HIGH)
    state_in = earlier_states(through, last_state, seq_strides)
    skip_wide = jnp.dot(
        jnp.pad(lax.dynamic_slice_in_dim(skip_gain, head_start, head_count), pad_heads)[None, :],
        spread_f,
        precision=HIGH,
    )
    gain_local = lax.dynamic_slice_in_dim(gated_gain, col_start, local_width)
    rows_wide = jnp.concatenate(
        [skip_wide, gain_local[None, :], jnp.zeros((6, local_width), F32)], axis=0
    )
    full_y, scaled_low, mixer_part, squares = pl.pallas_call(
        gate_forward,
        grid=(span_count,),
        in_specs=[
            tile(local_width),
            tile(LANES),
            tile(pair_width),
            whole(state_dim, local_width),
            tile(local_width),
            tile(local_width),
            whole(8, local_width),
            whole(LANES, local_width),
            whole(model_width, local_width),
        ],
        out_specs=[tile(local_width), tile(local_width), tile(model_width), tile(1)],
        out_shape=[
            shape((length, local_width), F32),
            shape((length, local_width), BF16),
            shape((length, model_width), BF16),
            shape((length, 1), F32),
        ],
        compiler_params=compiler_params(),
        cost_estimate=cost(
            2 * length * local_width * (model_width + 3 * LANES),
            length * (local_width * 16 + model_width * 2),
        ),
        name="gate_forward",
    )(local_y, reach, bc_low, state_in, inputs, gate_z, rows_wide, spread, weight_out)

    mixer_rows = scatter_exp(mixer_part.reshape(exp_count, rows_here, model_width), exp_strides)
    square_rows = scatter_exp(squares.reshape(exp_count, 1, rows_here), exp_strides)
    square_rows = square_rows.reshape(rows_here, 1)
    scale_mix = lax.rsqrt(square_rows / inner_width + EPS)
    residual = (
        lax.dynamic_slice_in_dim(tokens, exp_pos * rows_here, rows_here).astype(F32)
        + scale_mix * mixer_rows
    )
    scale_mid = rms_scale(residual)
    normed_mid = residual * scale_mid
    mid_low = (normed_mid * norm_mid[None, :]).astype(BF16)
    mid_all = gather_group(mid_low, steps_group)

    got = dispatch(mid_all, place_rows, capacity)
    place_here = jnp.reshape(seq_pos, (1,)).astype(jnp.int32)
    expert_hid, grad_a, grad_b, expert_res, grad_rows = run_experts(
        place_here, got, grad_got, gate_pieces, up_pieces, down_pieces
    )
    shared_ab = low_dot(mid_all, shared_in)
    shared_a, shared_b = shared_ab[:, :hidden_part], shared_ab[:, hidden_part:]
    shared_hid = (jax.nn.silu(shared_a) * shared_b).astype(BF16)
    grad_ab = jnp.concatenate(
        [grad_shid * shared_b * silu_slope(shared_a), grad_shid * jax.nn.silu(shared_a)], axis=1
    ).astype(BF16)
    grad_mid = scatter_group(
        combine(grad_rows, place_cols, grad_ab, shared_in, True), steps_group
    )
    routed = scatter_group(
        combine(expert_res, place_cols, shared_hid, shared_back, False, gate_cols), steps_group
    )
    block_output = (residual + routed).astype(BF16)
    grad_pieces = expert_grads(
        place_here, got, grad_got, expert_hid, grad_a, grad_b, seq_count
    )
    sum_gate_e, sum_up_e, sum_down_e = [
        collect_weights(pieces, low_z, weight_strides) for pieces in grad_pieces
    ]
    sum_down_e = sum_down_e.transpose(0, 2, 1)
    shared_grads = jnp.concatenate(
        [dot_tn(grad_ab, mid_all), dot_tn(shared_hid, cot_all)], axis=0
    ).astype(BF16)

    grad_norm_mid = jnp.sum(grad_mid * normed_mid, axis=0)
    grad_resid = cotangent.astype(F32) + norm_back(grad_mid, norm_mid, normed_mid, scale_mid)
    grad_part = (scale_mix * grad_resid).astype(BF16)
    grad_square = (
        jnp.sum(grad_resid * mixer_rows, axis=1, keepdims=True) * -0.5 * scale_mix**3 / inner_width
    ).astype(BF16)
    grad_part_all = gather_exp(grad_part, exp_strides)
    grad_square_all = gather_exp(grad_square.reshape(1, rows_here), exp_strides)
    grad_square_all = grad_square_all.astype(F32).reshape(length, 1)

    grad_y, grad_z, gate_sums, direct = pl.pallas_call(
        gate_backward,
        grid=(span_count,),
        in_specs=[
            tile(model_width),
            tile(1),
            tile(local_width),
            tile(local_width),
            tile(local_width),
            tile(LANES),
            tile(pair_width),
            whole(8, local_width),
            whole(LANES, local_width),
            whole(model_width, local_width),
        ],
        out_specs=[
            tile(local_width),
            tile(local_width),
            whole(8, local_width),
            whole(state_dim, local_width),
        ],
        out_shape=[
            shape((length, local_width), BF16),
            shape((length, local_width), BF16),
            shape((8, local_width), F32),
            shape((state_dim, local_width), F32),
        ],
        compiler_params=compiler_params(),
        cost_estimate=cost(
            2 * length * local_width * (model_width + 3 * LANES),
            length * (local_width * 16 + model_width * 2),
        ),
        name="gate_backward",
    )(
        grad_part_all,
        grad_square_all,
        full_y,
        gate_z,
        inputs,
        reach,
        bc_low,
        rows_wide,
        spread,
        weight_out,
    )
    state_grad = later_grads(through, direct, seq_strides)
    sum_wout = lax.psum_scatter(
        dot_tn(grad_part_all, scaled_low).astype(BF16), "seq", scatter_dimension=0, tiled=True
    ).astype(F32).T
    sum_wz = lax.psum_scatter(
        dot_tn(in_low, grad_z).astype(BF16), "seq", scatter_dimension=0, tiled=True
    ).astype(F32)

    passed = jnp.concatenate([jnp.ones((1, LANES), F32), reach[SPAN - 1 : length - 1 : SPAN]])
    passed = jnp.broadcast_to(passed[:, None, :], (span_count, 8, LANES))
    turn = lambda i: span_count - 1 - i
    ahead = SPAN // 8
    before_tile = lambda cols: pl.BlockSpec(
        (8, cols), lambda i: (jnp.maximum(turn(i) * ahead - 1, 0), 0)
    )
    grad_x, grad_bc, grad_steps, tail_rows, head_rows, conv_sums, rate_sums = pl.pallas_call(
        scan_backward,
        grid=(span_count,),
        in_specs=[
            tile(channels, turn),
            tile(local_width, turn),
            tile(raw_s.shape[1], turn),
            before_tile(local_width),
            before_tile(raw_s.shape[1]),
            whole(8, channels),
            tile(8, turn),
            seg_tile(turn),
            whole(8, channels),
            tile(LANES, turn),
            whole(8, LANES),
            whole(LANES, local_width),
            whole(local_width, LANES),
            tile(local_width, turn),
            tile(pair_width, turn),
            tile(local_width, turn),
            tile(local_width, turn),
            pl.BlockSpec((1, state_dim, local_width), lambda i: (turn(i), 0, 0)),
            pl.BlockSpec((1, 8, LANES), lambda i: (turn(i), 0, 0)),
            whole(state_dim, local_width),
            whole(state_dim, local_width),
            whole(8, local_width),
        ],
        out_specs=[
            tile(local_width, turn),
            tile(pair_width, turn),
            tile(LANES, turn),
            whole(8, channels),
            whole(8, channels),
            whole(8, channels),
            whole(8, LANES),
        ],
        out_shape=[
            shape((length, local_width), BF16),
            shape((length, pair_width), BF16),
            shape((length, LANES), F32),
            shape((8, channels), F32),
            shape((8, channels), F32),
            shape((8, channels), F32),
            shape((8, LANES), F32),
        ],
        scratch_shapes=[pltpu.VMEM((SPAN + 8, channels), F32)] * 4
        + [pltpu.VMEM((state_dim, local_width), F32), pltpu.VMEM((local_width, SPAN), F32)],
        compiler_params=compiler_params(),
        cost_estimate=cost(
            10 * elements * LANES, length * (channels * 16 + local_width * 16 + 4096), elements
        ),
        name="scan_backward",
    )(
        conv_out,
        raw_x,
        raw_s,
        raw_x,
        raw_s,
        halo,
        marks,
        seg_rows,
        taps,
        step_sizes,
        heads,
        spread,
        spread.T,
        inputs,
        bc_low,
        full_y,
        grad_y,
        entries,
        passed,
        state_in,
        state_grad,
        rows_wide,
    )
    edge = jnp.stack(
        [
            sum(
                taps[tap] * marks[at - tap, tap] * head_rows[at - tap]
                for tap in range(at + 1)
            )
            for at in range(CONV - 1)
        ]
    )
    edge_back = lax.ppermute(edge, "seq", [(i + 1, i) for i in range(seq_count - 1)])
    tail_fixed = tail_rows + jnp.pad(edge_back, ((8 - (CONV - 1), 0), (0, 0)))
    grad_x = grad_x.at[length - 8 :].set(tail_fixed[:, :local_width].astype(BF16))
    grad_bc = grad_bc.at[length - 8 :].set(tail_fixed[:, local_width:].astype(BF16))
    grad_dt_raw = grad_steps * jax.nn.sigmoid(raw_dt) * lane_on.astype(F32)[None, :]
    grad_dt = grad_dt_raw.astype(BF16)
    grad_in = (
        dot_nt(grad_z, weight_z)
        + dot_nt(grad_x, weight_x)
        + dot_nt(grad_dt, weight_dt)
        + dot_nt(grad_bc, proj_bc)
    )
    grad_wxdt = jnp.concatenate([dot_tn(in_low, grad_x), dot_tn(in_low, grad_dt)], axis=1)
    sum_wxdt = lax.psum_scatter(
        grad_wxdt.astype(BF16), "seq", scatter_dimension=0, tiled=True
    ).astype(F32)
    grad_wbc = dot_tn(in_low, grad_bc)
    normed_in = tokens_f * scale_in
    grad_norm_in = jnp.sum(grad_in * normed_in, axis=0)
    grad_in_part = norm_back(grad_in, norm_in, normed_in, scale_in).astype(BF16)
    tokens_grad = grad_resid + scatter_exp(
        grad_in_part.reshape(exp_count, rows_here, model_width), exp_strides
    )

    quarter = scatter_rows(shared_grads, "seq", bits(low_z) + [2 * low_z])
    pieces = lax.all_gather(quarter, ("seq", "exp"), axis=0, tiled=True)
    part_rows = quarter.shape[0]
    pieces = pieces.reshape(2, 2, low_z, exp_count, part_rows, model_width)
    pieces = pieces.transpose(1, 3, 0, 2, 4, 5).reshape(
        block_count, 3, hidden_part, model_width
    )
    pieces = pieces.transpose(1, 0, 2, 3).reshape(3, block_count * hidden_part, model_width)
    pieces = pieces.astype(F32)

    def placed_cols(values, total, start):
        blank = jnp.zeros(values.shape[:-1] + (total,), F32)
        return lax.dynamic_update_slice_in_dim(blank, values, start, values.ndim - 1)

    def placed_conv(values):
        mine = placed_cols(values[..., :local_width], inner_width, col_start)
        return jnp.concatenate([mine, values[..., local_width:]], axis=-1)

    def placed_heads(values):
        return placed_cols(values[:head_count], head_total, head_start)

    skip_sums = jnp.dot(gate_sums[1:2], spread_f.T, precision=HIGH)[0]
    summed = lax.psum(
        (
            grad_norm_in,
            grad_wbc,
            placed_conv(conv_sums[:CONV]),
            placed_conv(conv_sums[CONV]),
            placed_heads(jnp.sum(grad_dt_raw, axis=0)),
            placed_heads(rate_sums[0] * rates_local),
            placed_heads(skip_sums),
            placed_cols(gate_sums[0], inner_width, col_start),
            grad_norm_mid,
        ),
        ("seq", "exp"),
    )
    return (
        block_output,
        tokens_grad,
        summed[0],
        sum_wz,
        sum_wxdt[:, :local_width],
        summed[1],
        sum_wxdt[:, local_width : local_width + head_count],
        summed[2],
        summed[3],
        summed[4],
        summed[5],
        summed[6],
        summed[7],
        sum_wout,
        summed[8],
        sum_gate_e,
        sum_up_e,
        sum_down_e,
        pieces[0].T,
        pieces[1].T,
        pieces[2],
    )


def solution(mesh):
    placed = (
        P("seq", None),
        P(),
        P(("seq", "exp"), None),
        P(("seq", "exp"), None),
        P(("seq", "exp"), None),
        P(),
        P("seq", "exp"),
        P("seq", "exp"),
        P(),
        P("seq", "exp"),
        P(),
        P(),
        P(),
        P(),
        P(),
        P(),
        P("exp", "seq"),
        P(),
        P("exp", "seq", None),
        P("exp", "seq", None),
        P("exp", None, "seq"),
        P(),
        P(),
        P(),
    )
    return jax.shard_map(
        per_device,
        mesh=mesh,
        in_specs=placed,
        out_specs=(
            P(("seq", "exp"), None),
            P(("seq", "exp"), None),
            P(),
            P("seq", "exp"),
            P("seq", "exp"),
            P(),
            P("seq", "exp"),
            P(),
            P(),
            P(),
            P(),
            P(),
            P(),
            P("exp", "seq"),
            P(),
            P("exp", "seq", None),
            P("exp", "seq", None),
            P("exp", None, "seq"),
            P(),
            P(),
            P(),
        ),
        check_vma=False,
    )
```

```python
from functools import partial

import jax
import jax.numpy as jnp
from jax import lax
from jax.experimental import pallas as pl
from jax.experimental.pallas import tpu as pltpu
from jax.sharding import Mesh
from jax.sharding import PartitionSpec as P

CONV = 4
SPAN = 256
LANES = 128
EPS = 1e-05
FLOOR = -1e30
HIGH = lax.Precision.HIGHEST
SEQ = ("far", "near", "low")
GROUP = ("far", "exp")
ALL = SEQ + ("exp",)
VMEM_BYTES = 56 * 1024 * 1024
F32 = jnp.float32
BF16 = jnp.bfloat16


def low_dot(left, right):
    return jnp.dot(left, right, preferred_element_type=F32)


def dot_nt(left, right):
    return lax.dot_general(left, right, (((1,), (1,)), ((), ())), preferred_element_type=F32)


def dot_tn(left, right):
    return lax.dot_general(left, right, (((0,), (0,)), ((), ())), preferred_element_type=F32)


def split_dot(values, table):
    high = values.astype(BF16)
    rest = (values - high.astype(F32)).astype(BF16)
    return low_dot(high, table) + low_dot(rest, table)


def exact_sum(triangle, values):
    high = values.astype(BF16)
    rest = values - high.astype(F32)
    middle = rest.astype(BF16)
    small = (rest - middle.astype(F32)).astype(BF16)
    return low_dot(triangle, high) + low_dot(triangle, middle) + low_dot(triangle, small)


def silu_slope(values):
    sigmoid_v = jax.nn.sigmoid(values)
    return sigmoid_v * (1.0 + values * (1.0 - sigmoid_v))


def rms_scale(values):
    return lax.rsqrt(jnp.mean(values * values, axis=-1, keepdims=True) + EPS)


def norm_back(grad_normed, gain, normed, scale):
    weighted = grad_normed * gain[None, :]
    return scale * (weighted - normed * jnp.mean(weighted * normed, axis=-1, keepdims=True))


def compiler_params(steps=1):
    return pltpu.CompilerParams(
        dimension_semantics=("arbitrary",) * steps, vmem_limit_bytes=VMEM_BYTES
    )


def cost(flops, moved, exps=0):
    return pl.CostEstimate(flops=int(flops), bytes_accessed=int(moved), transcendentals=int(exps))


def causal(span):
    rows = lax.broadcasted_iota(jnp.int32, (span, span), 0)
    cols = lax.broadcasted_iota(jnp.int32, (span, span), 1)
    return rows >= cols


def span_terms(steps, marks, seg_row, rates, b_low, c_low):
    span = steps.shape[0]
    keep = causal(span)
    cum = exact_sum(keep.astype(F32).astype(BF16), steps * rates)
    cum_rows = cum.T
    same = marks[:, 6:7] == seg_row
    bias = jnp.where(keep & same, 0.0, FLOOR)
    scores = dot_nt(c_low, b_low)
    last = cum[span - 1 : span, :]
    entry = jnp.exp(cum) * marks[:, 4:5]
    tail = jnp.exp(last - cum) * marks[:, 5:6]
    return cum, cum_rows, bias, scores, last, entry, tail


def scan_forward(
    raw_x,
    raw_s,
    halo,
    marks,
    seg_row,
    taps,
    steps,
    heads,
    spread,
    conv_out,
    x_out,
    bc_out,
    y_out,
    reach_out,
    entries_out,
    last_out,
    ext,
    state,
    total,
):
    turn = pl.program_id(0)
    span, width = raw_x.shape
    channels = taps.shape[1]

    @pl.when(turn == 0)
    def _():
        ext[0:8, :] = halo[...]
        state[...] = jnp.zeros_like(state)
        total[...] = jnp.zeros_like(total)

    @pl.when(turn > 0)
    def _():
        ext[0:8, :] = ext[span : span + 8, :]

    ext[8 : 8 + span, 0:width] = raw_x[...]
    ext[8 : 8 + span, width:channels] = raw_s[:, 0 : channels - width]
    mark = marks[...]
    for start in range(0, channels, LANES):
        cols = slice(start, start + LANES)
        conv = taps[4:5, cols] + taps[3:4, cols] * ext[8 : 8 + span, cols]
        for tap in range(CONV - 1):
            conv = conv + taps[tap : tap + 1, cols] * (
                ext[5 + tap : 5 + tap + span, cols] * mark[:, tap : tap + 1]
            )
        conv_out[:, cols] = conv
        act = (conv * jax.nn.sigmoid(conv)).astype(BF16)
        if start < width:
            x_out[:, cols] = act
        else:
            bc_out[:, start - width : start - width + LANES] = act
    half = (channels - width) // 2
    b_low = bc_out[:, 0:half]
    c_low = bc_out[:, half:]
    step = steps[...]
    rates = heads[1:2, :]
    cum, cum_rows, bias, scores, last, entry, tail = span_terms(
        step, mark, seg_row[0], rates, b_low, c_low
    )
    reach_out[...] = jnp.exp(cum + total[0:1, :]) * mark[:, 3:4]
    total[0:1, :] = total[0:1, :] + last
    table = spread[...]
    entry_wide = split_dot(entry, table)
    xf = x_out[...].astype(F32)
    fed = (xf * split_dot(step, table)).astype(BF16)
    kept = (xf * split_dot(tail * step, table)).astype(BF16)
    entries_out[0] = state[...]
    state_low = state[...].astype(BF16)
    y_out[...] = entry_wide * low_dot(c_low, state_low)
    left_half = lax.broadcasted_iota(jnp.int32, (span, LANES), 1) < LANES // 2
    for pair in range(width // LANES):
        cols = slice(pair * LANES, (pair + 1) * LANES)
        both = []
        for head in (2 * pair, 2 * pair + 1):
            decay = jnp.exp(cum[:, head : head + 1] - cum_rows[head : head + 1, :] + bias)
            both.append(low_dot((decay * scores).astype(BF16), fed[:, cols]))
        y_out[:, cols] = y_out[:, cols] + jnp.where(left_half, both[0], both[1])
    state[...] = state[...] * entry_wide[span - 1 : span, :] + dot_tn(b_low, kept)

    @pl.when(turn == pl.num_programs(0) - 1)
    def _():
        last_out[...] = state[...]


def gate_forward(
    y_local,
    reach,
    bc,
    state_in,
    x,
    gate,
    rows,
    spread,
    weight,
    full_out,
    low_out,
    mixer_out,
    square_out,
):
    half = bc.shape[1] // 2
    c_low = bc[:, half:]
    far = split_dot(reach[...], spread[...]) * low_dot(c_low, state_in[...].astype(BF16))
    full = y_local[...] + far + rows[0:1, :] * x[...].astype(F32)
    full_out[...] = full
    z = gate[...]
    gated = full * (z * jax.nn.sigmoid(z))
    square_out[...] = jnp.sum(gated * gated, axis=1, keepdims=True)
    low = (gated * rows[1:2, :]).astype(BF16)
    low_out[...] = low
    mixer_out[...] = dot_nt(low, weight[...]).astype(BF16)


def gate_backward(
    part_grad,
    square_grad,
    full_y,
    gate,
    x,
    reach,
    bc,
    rows,
    spread,
    weight,
    grad_y_out,
    grad_z_out,
    sums_out,
    direct_out,
):
    turn = pl.program_id(0)
    z = gate[...]
    sig = jax.nn.sigmoid(z)
    act = z * sig
    full = full_y[...]
    gated = full * act
    scaled_grad = low_dot(part_grad[...], weight[...])
    gated_grad = scaled_grad * rows[1:2, :] + 2.0 * gated * square_grad[...]
    grad_full = gated_grad * act
    grad_y_out[...] = grad_full.astype(BF16)
    grad_z_out[...] = (gated_grad * full * (sig * (1.0 + z * (1.0 - sig)))).astype(BF16)
    half = bc.shape[1] // 2
    seen = (grad_full * split_dot(reach[...], spread[...])).astype(BF16)
    direct = dot_tn(bc[:, half:], seen)
    gain_sum = jnp.sum(scaled_grad * gated, axis=0, keepdims=True)
    skip_sum = jnp.sum(grad_full * x[...].astype(F32), axis=0, keepdims=True)

    @pl.when(turn == 0)
    def _():
        sums_out[...] = jnp.zeros_like(sums_out)
        direct_out[...] = jnp.zeros_like(direct_out)

    sums_out[0:1, :] = sums_out[0:1, :] + gain_sum
    sums_out[1:2, :] = sums_out[1:2, :] + skip_sum
    direct_out[...] = direct_out[...] + direct


def scan_backward(
    conv,
    raw_x,
    raw_s,
    raw_x_before,
    raw_s_before,
    halo,
    marks,
    seg_row,
    taps,
    steps,
    heads,
    spread,
    fold,
    x,
    bc,
    full_y,
    grad_y,
    entries,
    passed,
    state_in,
    state_grad,
    rows,
    grad_x_out,
    grad_bc_out,
    grad_step_out,
    tail_out,
    head_out,
    sums_out,
    rates_out,
    ext,
    later0,
    later1,
    later2,
    back,
    turned,
):
    turn = pl.program_id(0)
    span, width = raw_x.shape
    channels = taps.shape[1]
    half = (channels - width) // 2
    later = (later0, later1, later2)

    @pl.when(turn == 0)
    def _():
        back[...] = state_grad[...]
        sums_out[...] = jnp.zeros_like(sums_out)
        rates_out[...] = jnp.zeros_like(rates_out)
        for kept in later:
            kept[span : span + 8, :] = jnp.zeros((8, channels), F32)

    @pl.when(turn > 0)
    def _():
        for kept in later:
            kept[span : span + 8, :] = kept[0:8, :]

    @pl.when(turn == pl.num_programs(0) - 1)
    def _():
        ext[0:8, :] = halo[...]

    @pl.when(turn < pl.num_programs(0) - 1)
    def _():
        ext[0:8, 0:width] = raw_x_before[...]
        ext[0:8, width:channels] = raw_s_before[:, 0 : channels - width]

    ext[8 : 8 + span, 0:width] = raw_x[...]
    ext[8 : 8 + span, width:channels] = raw_s[:, 0 : channels - width]
    mark = marks[...]
    step = steps[...]
    rates = heads[1:2, :]
    b_low = bc[:, 0:half]
    c_low = bc[:, half:]
    cum, cum_rows, bias, scores, last, entry, tail = span_terms(
        step, mark, seg_row[0], rates, b_low, c_low
    )
    table = spread[...]
    entry_wide = split_dot(entry, table)
    tail_wide = split_dot(tail, table)
    step_wide = split_dot(step, table)
    xf = x[...].astype(F32)
    fed_low = (xf * step_wide).astype(BF16)
    fed = fed_low.astype(F32)
    dy_low = grad_y[...]
    dy = dy_low.astype(F32)
    seen = (dy * entry_wide).astype(BF16)
    entered = entries[0] + split_dot(passed[0], table)[0:1, :] * state_in[...]
    entered_low = entered.astype(BF16)
    back_low = back[...].astype(BF16)
    turned_dy = dy.T.astype(BF16)
    left_half = lax.broadcasted_iota(jnp.int32, (span, LANES), 1) < LANES // 2
    score_grad = jnp.zeros((span, span), F32)
    head_rows = LANES // 2
    for pair in range(width // LANES):
        cols = slice(pair * LANES, (pair + 1) * LANES)
        fed_pair = fed_low[:, cols]
        dy_pair = dy[:, cols]
        for side in (0, 1):
            head = 2 * pair + side
            decay = jnp.exp(cum[:, head : head + 1] - cum_rows[head : head + 1, :] + bias)
            weights = (decay * scores).astype(BF16)
            own = jnp.where(left_half if side == 0 else ~left_half, dy_pair, 0.0).astype(BF16)
            score_grad = score_grad + dot_nt(own, fed_pair) * decay
            lanes = slice(head * head_rows, (head + 1) * head_rows)
            turned[lanes, :] = low_dot(turned_dy[lanes, :], weights)
    score_low = score_grad.astype(BF16)
    inner = turned[...].T
    far = tail_wide * low_dot(b_low, back_low)
    fed_grad = inner + far
    skip = rows[0:1, :]
    scan_y = full_y[...] - skip * xf
    summed = fold[...]
    far_sums = split_dot(fed * far, summed)
    kept_row = jnp.sum(back[...] * entered, axis=0, keepdims=True) * entry_wide[span - 1 : span, :]
    kept_sum = split_dot(jnp.broadcast_to(kept_row, (8, width)), summed)[0:1, :]
    log_grad = split_dot(dy * scan_y - fed * fed_grad, summed)
    ends = jnp.sum(far_sums, axis=0, keepdims=True) + kept_sum
    rows_i = lax.broadcasted_iota(jnp.int32, (span, span), 0)
    cols_i = lax.broadcasted_iota(jnp.int32, (span, span), 1)
    upper = (cols_i >= rows_i).astype(F32).astype(BF16)
    rate_step_grad = exact_sum(upper, log_grad) + ends
    grad_step_out[...] = split_dot(fed_grad * xf, summed) + rates * rate_step_grad
    rates_out[0:1, :] = rates_out[0:1, :] + jnp.sum(rate_step_grad * step, axis=0, keepdims=True)
    c_grad = dot_nt(seen, entered_low) + low_dot(score_low, b_low)
    b_grad = dot_nt((fed * tail_wide).astype(BF16), back_low) + dot_tn(score_low, c_low)
    back[...] = back[...] * entry_wide[span - 1 : span, :] + dot_tn(c_low, seen)
    x_grad = fed_grad * step_wide + skip * dy
    for start in range(0, channels, LANES):
        cols = slice(start, start + LANES)
        if start < width:
            active = x_grad[:, cols]
        elif start < width + half:
            active = b_grad
        else:
            active = c_grad
        grad = active * silu_slope(conv[:, cols])

        @pl.when(turn == pl.num_programs(0) - 1)
        def _():
            head_out[:, cols] = grad[0:8, :]

        source = taps[3:4, cols] * grad
        sums_out[4:5, cols] = sums_out[4:5, cols] + jnp.sum(grad, axis=0, keepdims=True)
        sums_out[3:4, cols] = sums_out[3:4, cols] + jnp.sum(
            grad * ext[8 : 8 + span, cols], axis=0, keepdims=True
        )
        for tap in range(CONV - 1):
            masked = grad * mark[:, tap : tap + 1]
            later[tap][0:span, cols] = masked
            sums_out[tap : tap + 1, cols] = sums_out[tap : tap + 1, cols] + jnp.sum(
                masked * ext[5 + tap : 5 + tap + span, cols], axis=0, keepdims=True
            )
            shift = CONV - 1 - tap
            source = source + taps[tap : tap + 1, cols] * later[tap][shift : shift + span, cols]
        if start < width:
            grad_x_out[:, cols] = source.astype(BF16)
        else:
            grad_bc_out[:, start - width : start - width + LANES] = source.astype(BF16)

        @pl.when(turn == 0)
        def _():
            tail_out[:, cols] = source[span - 8 : span, :]


def dispatch_kernel(weighted, *refs):
    if weighted:
        rows, places, gates, out = refs
    else:
        rows, places, out = refs
    experts, _, slots, _ = out.shape
    count = rows.shape[0]
    slot = lax.broadcasted_iota(jnp.int32, (slots, count), 0)
    hits = [slot == places[0, e : e + 1, :] for e in range(experts)]
    chosen = jnp.concatenate([hit.astype(F32).astype(BF16) for hit in hits], axis=0)
    taken = low_dot(chosen, rows[...])
    for e in range(experts):
        part = taken[e * slots : (e + 1) * slots, :]
        if weighted:
            part = part * jnp.sum(
                jnp.where(hits[e], gates[0, e : e + 1, :], 0.0), axis=1, keepdims=True
            )
        out[e, 0] = part.astype(BF16)


def dispatch(rows, places, slots, width, gates=None, here=None):
    blocks, experts, count = places.shape
    arrays = (rows, places) if gates is None else (rows, places, gates)
    kernel = partial(dispatch_kernel, gates is not None)
    here = jnp.zeros((1,), jnp.int32) if here is None else here
    small = pl.BlockSpec((1, experts, count), lambda b, here: (b, 0, 0))
    return pl.pallas_call(
        lambda here, *refs: kernel(*refs),
        grid_spec=pltpu.PrefetchScalarGridSpec(
            num_scalar_prefetch=1,
            grid=(blocks,),
            in_specs=[pl.BlockSpec((count, width), lambda b, here: (b ^ here[0], 0))]
            + [small] * (len(arrays) - 1),
            out_specs=pl.BlockSpec(
                (experts, 1, slots, width), lambda b, here: (0, b, 0, 0)
            ),
        ),
        out_shape=jax.ShapeDtypeStruct((experts, blocks, slots, width), BF16),
        compiler_params=compiler_params(),
        cost_estimate=cost(
            2 * blocks * experts * slots * count * width,
            2 * blocks * count * width + 2 * experts * blocks * slots * width,
        ),
        name="dispatch",
    )(here, *arrays)


def expert_kernel(pieces, me, got, grad_got, *refs):
    weights = refs[:pieces]
    hid_out, grads_out, res_out, row_out, full = refs[pieces:]
    part = weights[0].shape[-2]
    hidden = hid_out.shape[2]
    for piece, ref in enumerate(weights):
        start = pl.multiple_of((me[0] ^ piece) * part, part)
        full[pl.ds(start, part), :] = ref[0]
    gate, up, down = (slice(kind * hidden, (kind + 1) * hidden) for kind in range(3))
    blocks, slots, width = got.shape[1:]
    step = max(1, min(blocks, 384 // slots))
    for first in range(0, blocks, step):
        rows = slice(first * slots, (first + step) * slots)
        taken = got[0, first : first + step].reshape(step * slots, width)
        taken_grad = grad_got[0, first : first + step].reshape(step * slots, width)
        a = low_dot(taken, full[:, gate])
        b = low_dot(taken, full[:, up])
        hid_grad = low_dot(taken_grad, full[:, down])
        sig = jax.nn.sigmoid(a)
        act = a * sig
        hid = (act * b).astype(BF16)
        a_grad = (hid_grad * b * (sig * (1.0 + a * (1.0 - sig)))).astype(BF16)
        b_grad = (hid_grad * act).astype(BF16)
        hid_out[0, rows, :] = hid
        grads_out[0, rows, 0:hidden] = a_grad
        grads_out[0, rows, hidden:] = b_grad
        res = dot_nt(hid, full[:, down]).astype(BF16)
        row = (dot_nt(a_grad, full[:, gate]) + dot_nt(b_grad, full[:, up])).astype(BF16)
        res_out[0, first : first + step] = res.reshape(step, slots, width)
        row_out[0, first : first + step] = row.reshape(step, slots, width)


def run_experts(me, got, grad_got, pieces):
    count, blocks, slots, width = got.shape
    part, packed = pieces[0].shape[1:]
    hidden = packed // 3
    total = blocks * slots
    wide = pl.BlockSpec((1, blocks, slots, width), lambda e, me: (e, 0, 0, 0))
    narrow = pl.BlockSpec((1, total, hidden), lambda e, me: (e, 0, 0))
    double = pl.BlockSpec((1, total, 2 * hidden), lambda e, me: (e, 0, 0))
    piece = pl.BlockSpec((1, part, packed), lambda e, me: (e, 0, 0))
    shape = jax.ShapeDtypeStruct
    row_shape = shape((count, blocks, slots, width), BF16)
    return pl.pallas_call(
        partial(expert_kernel, len(pieces)),
        grid_spec=pltpu.PrefetchScalarGridSpec(
            num_scalar_prefetch=1,
            grid=(count,),
            in_specs=[wide, wide] + [piece] * len(pieces),
            out_specs=[narrow, double, wide, wide],
            scratch_shapes=[pltpu.VMEM((width, packed), BF16)],
        ),
        out_shape=[
            shape((count, total, hidden), BF16),
            shape((count, total, 2 * hidden), BF16),
            row_shape,
            row_shape,
        ],
        compiler_params=compiler_params(),
        cost_estimate=cost(
            12 * count * total * width * hidden,
            count * (8 * total * width + 6 * width * hidden),
            count * total * hidden,
        ),
        name="experts",
    )(me, got, grad_got, *pieces)


def expert_grad_kernel(pieces, me, got, grad_got, hid, grads, *refs):
    outs, full = refs[:pieces], refs[pieces]
    blocks, slots, width = got.shape[1:]
    part = outs[0].shape[1]
    hidden = hid.shape[2]
    total = blocks * slots
    step = 256
    for start in range(0, width, step):
        cols = slice(start, start + step)
        taken = got[0, :, :, cols].reshape(total, step)
        taken_grad = grad_got[0, :, :, cols].reshape(total, step)
        full[cols, 0 : 2 * hidden] = dot_tn(taken, grads[0]).astype(BF16)
        full[cols, 2 * hidden :] = dot_tn(taken_grad, hid[0]).astype(BF16)
    for piece in range(pieces):
        start = pl.multiple_of((me[0] ^ piece) * part, part)
        outs[piece][0] = full[pl.ds(start, part), :]


def expert_grads(me, got, grad_got, hid, grads, pieces):
    count, blocks, slots, width = got.shape
    total, hidden = hid.shape[1:]
    part = width // pieces
    packed = 3 * hidden
    wide = pl.BlockSpec((1, blocks, slots, width), lambda e, me: (e, 0, 0, 0))
    narrow = pl.BlockSpec((1, total, hidden), lambda e, me: (e, 0, 0))
    double = pl.BlockSpec((1, total, 2 * hidden), lambda e, me: (e, 0, 0))
    piece = pl.BlockSpec((1, part, packed), lambda e, me: (e, 0, 0))
    return pl.pallas_call(
        partial(expert_grad_kernel, pieces),
        grid_spec=pltpu.PrefetchScalarGridSpec(
            num_scalar_prefetch=1,
            grid=(count,),
            in_specs=[wide] * 2 + [narrow, double],
            out_specs=[piece] * pieces,
            scratch_shapes=[pltpu.VMEM((width, packed), BF16)],
        ),
        out_shape=[jax.ShapeDtypeStruct((count, part, packed), BF16)] * pieces,
        compiler_params=compiler_params(),
        cost_estimate=cost(
            6 * count * total * width * hidden, count * (4 * total * width + 6 * width * hidden)
        ),
        name="expert_grads",
    )(me, got, grad_got, hid, grads)


def owner_kernel(count, me, *refs):
    arrived, outs = refs[:2], refs[2:]
    hidden = arrived[0].shape[2] // 3
    turn = pl.program_id(0)
    for place, values in enumerate(arrived):

        @pl.when(turn // count == me[0] ^ place)
        def _():
            full = values[0].astype(F32)
            outs[0][0] = full[:, :hidden]
            outs[1][0] = full[:, hidden : 2 * hidden]
            outs[2][0] = full[:, 2 * hidden :].T


def owner_grads(me, arrived):
    count, part, packed = arrived[0].shape
    hidden = packed // 3
    shape = jax.ShapeDtypeStruct
    one = lambda rows, cols: pl.BlockSpec((1, rows, cols), lambda e, me: (e, 0, 0))
    return pl.pallas_call(
        partial(owner_kernel, count),
        grid_spec=pltpu.PrefetchScalarGridSpec(
            num_scalar_prefetch=1,
            grid=(2 * count,),
            in_specs=[pl.BlockSpec((1, part, packed), lambda e, me: (e % count, 0, 0))] * 2,
            out_specs=[one(part, hidden), one(part, hidden), one(hidden, part)],
        ),
        out_shape=[shape((2 * count, part, hidden), F32)] * 2
        + [shape((2 * count, hidden, part), F32)],
        compiler_params=compiler_params(),
        cost_estimate=cost(0, 12 * count * part * packed),
        name="owner_grads",
    )(me, *arrived)


def combine_kernel(weighted, turned, *refs):
    if weighted:
        rows, places, table, number, gates, hidden, weight, out = refs
    else:
        rows, places, table, number, hidden, weight, out = refs
    experts, _, slots, width = rows.shape
    wide = low_dot(places[0], table[...])
    factor = low_dot(gates[0], table[...]) if weighted else 1.0
    chosen = jnp.where(wide == number[...], factor, 0.0).astype(BF16)
    total = low_dot(chosen, rows[:, 0].reshape(experts * slots, width))
    dense = dot_nt if turned else low_dot
    out[...] = (total + dense(hidden[...], weight[...])).astype(BF16)


def combine(rows, places, hidden, weight, turned, gates=None):
    experts, blocks, slots, width = rows.shape
    count = places.shape[1]
    expert_of = jnp.arange(experts * slots, dtype=jnp.int32) // slots
    table = (jnp.arange(experts, dtype=jnp.int32)[:, None] == expert_of[None, :]).astype(BF16)
    number = (jnp.arange(experts * slots, dtype=jnp.int32) % slots).astype(F32)[None, :]
    small = pl.BlockSpec((1, count, experts), lambda b: (b, 0, 0))
    arrays = [rows, places, table, number]
    specs = [
        pl.BlockSpec((experts, 1, slots, width), lambda b: (0, b, 0, 0)),
        small,
        pl.BlockSpec(table.shape, lambda b: (0, 0)),
        pl.BlockSpec(number.shape, lambda b: (0, 0)),
    ]
    if gates is not None:
        arrays.append(gates)
        specs.append(small)
    arrays += [hidden, weight]
    specs += [
        pl.BlockSpec((count, hidden.shape[1]), lambda b: (b, 0)),
        pl.BlockSpec(weight.shape, lambda b: (0, 0)),
    ]
    return pl.pallas_call(
        partial(combine_kernel, gates is not None, turned),
        grid=(blocks,),
        in_specs=specs,
        out_specs=pl.BlockSpec((count, width), lambda b: (b, 0)),
        out_shape=jax.ShapeDtypeStruct((blocks * count, width), BF16),
        compiler_params=compiler_params(),
        cost_estimate=cost(
            2 * blocks * count * width * (experts * slots + hidden.shape[1]),
            2 * blocks * experts * slots * width + 2 * blocks * count * width,
        ),
        name="combine",
    )(*arrays)


def swap(block, axis, stride):
    return lax.ppermute(
        block, axis, [(i, i ^ stride) for i in range(lax.axis_size(axis))]
    )


def bits(count):
    return [1 << i for i in range(count.bit_length() - 1)]


def bit_of(axis, stride):
    return (lax.axis_index(axis) // stride) % 2


def after(value, *earlier):
    return lax.optimization_barrier((value, earlier))[0]


def scatter_step(block, stride, left):
    left = list(reversed(bits(lax.axis_size(SEQ)))) if left is None else list(left)
    cols = block.shape[1]
    axis = left.index(stride)
    left.remove(stride)
    block = block.reshape((1 << axis, 2, -1, cols))
    place = bit_of(SEQ, stride)
    kept = lax.dynamic_index_in_dim(block, place, 1, False)
    sent = lax.dynamic_index_in_dim(block, 1 - place, 1, False)
    block = (kept.astype(F32) + swap(sent, SEQ, stride).astype(F32)).astype(block.dtype)
    return block.reshape(-1, cols), left


def sum_all(block, axis, strides):
    for stride in strides:
        block = block + swap(block, axis, stride)
    return block


def added(one, two):
    return (one.astype(F32) + two.astype(F32)).astype(BF16)


def gather_exp(block, strides):
    known = {0: block}
    for stride in strides:
        known.update({at | stride: swap(v, "exp", stride) for at, v in known.items()})
    for stride in strides:
        flipped = bit_of("exp", stride) == 1
        known = {at: jnp.where(flipped, known[at ^ stride], v) for at, v in known.items()}
    return jnp.concatenate([known[at] for at in range(len(known))], axis=0)


def scatter_exp(blocks, strides):
    place = lax.axis_index("exp")
    known = {
        at: lax.dynamic_index_in_dim(blocks, place ^ at, 0, False) for at in range(blocks.shape[0])
    }
    for stride in reversed(strides):
        known = {
            at: (v.astype(F32) + swap(known[at | stride], "exp", stride).astype(F32)).astype(
                F32 if len(known) == 2 else v.dtype
            )
            for at, v in known.items()
            if not at & stride
        }
    return known[0]


def split_rows(row):
    high = row.astype(BF16)
    rest = row - high.astype(F32)
    middle = rest.astype(BF16)
    return [high, middle, (rest - middle.astype(F32)).astype(BF16)]


def gather_states(through, state):
    rows = jnp.concatenate(split_rows(through), axis=0)
    packed = jnp.concatenate(
        [state.astype(BF16), jnp.pad(rows, ((0, 16 - rows.shape[0]), (0, 0)))], axis=0
    )
    gathered = lax.all_gather(packed, SEQ, axis=0).astype(F32)
    size = state.shape[0]
    return gathered[:, :size], jnp.sum(gathered[:, size : size + 3], axis=1, keepdims=True)


def earlier_states(states, decays):
    place = lax.axis_index(SEQ)
    total = jnp.zeros_like(states[0])
    for at in range(states.shape[0] - 1):
        total = jnp.where(at < place, states[at] + decays[at] * total, total)
    return total


def later_grads(grads, decays):
    place = lax.axis_index(SEQ)
    total = jnp.zeros_like(grads[0])
    for at in reversed(range(1, grads.shape[0])):
        total = jnp.where(at > place, grads[at] + decays[at] * total, total)
    return total


def per_device(
    tokens,
    segment_ids,
    routes,
    gate_weights,
    cotangent,
    norm_in,
    proj_z,
    proj_x,
    proj_bc,
    proj_dt,
    conv_weight,
    conv_bias,
    dt_bias,
    decay_log,
    skip_gain,
    gated_gain,
    proj_out,
    norm_mid,
    expert_gate,
    expert_up,
    expert_down,
    shared_gate,
    shared_up,
    shared_down,
):
    seq_pos = lax.axis_index(SEQ)
    exp_pos = lax.axis_index("exp")
    exp_count = lax.axis_size("exp")
    seq_count = lax.axis_size(SEQ)
    length, model_width = tokens.shape
    rows_here, top_count = routes.shape
    inner_width = gated_gain.shape[0]
    head_total = dt_bias.shape[0]
    pair_width = proj_bc.shape[1]
    state_dim = pair_width // 2
    local_width = proj_x.shape[1]
    head_count = proj_dt.shape[1]
    channels = local_width + pair_width
    col_start = exp_pos * local_width
    head_start = exp_pos * head_count
    low_z = seq_count // 4
    seq_strides = bits(seq_count)
    y_strides = bits(low_z)
    far_z = 2 * low_z
    exp_strides = list(reversed(bits(exp_count)))
    far_bit = bit_of(SEQ, far_z)
    block_count = 2 * exp_count
    span_count = length // SPAN

    pad_dt = jnp.pad(proj_dt, ((0, 0), (0, LANES - head_count)))
    projections = lax.all_gather(
        jnp.concatenate([proj_x, pad_dt, proj_z, proj_out.T], axis=1), SEQ, axis=0, tiled=True
    )
    weight_xdt = projections[:, : local_width + LANES]
    both = projections[:, local_width + LANES :]
    weight_x, weight_dt = weight_xdt[:, :local_width], weight_xdt[:, local_width:]
    halo_tokens = lax.ppermute(
        tokens[length - 8 :], SEQ, [(i, i + 1) for i in range(seq_count - 1)]
    )
    experts_here = expert_gate.shape[0]
    experts_half = experts_here // 2
    packed = jnp.concatenate(
        [expert_gate, expert_up, expert_down.transpose(0, 2, 1)], axis=2
    )
    kept = lax.dynamic_slice_in_dim(packed, far_bit * experts_half, experts_half, 0)
    sent = lax.dynamic_slice_in_dim(packed, (1 - far_bit) * experts_half, experts_half, 0)
    middle = experts_half // 2 if experts_half > 1 else experts_half
    low_0 = swap(kept, SEQ, 1)
    near_0 = swap(kept, SEQ, low_z)
    got_far = [swap(sent[:middle], SEQ, far_z)]

    hidden_part = shared_gate.shape[1] // block_count
    group_pos = far_bit * exp_count + exp_pos
    hidden_start = group_pos * hidden_part
    shared_in = jnp.concatenate(
        [
            lax.dynamic_slice_in_dim(shared_gate, hidden_start, hidden_part, 1),
            lax.dynamic_slice_in_dim(shared_up, hidden_start, hidden_part, 1),
        ],
        axis=1,
    )
    shared_back = lax.dynamic_slice_in_dim(shared_down, hidden_start, hidden_part, 0)

    tokens_f = tokens.astype(F32)
    scale_in = rms_scale(tokens_f)
    in_low = (tokens_f * scale_in * norm_in[None, :]).astype(BF16)
    halo_f = halo_tokens.astype(F32)
    halo_low = (halo_f * rms_scale(halo_f) * norm_in[None, :]).astype(BF16)
    raw_x = low_dot(in_low, weight_x)
    raw_s = low_dot(in_low, jnp.concatenate([proj_bc, weight_dt], axis=1))
    halo = jnp.concatenate([low_dot(halo_low, weight_x), low_dot(halo_low, proj_bc)], axis=1)
    padded_ids = jnp.concatenate([jnp.full((CONV - 1,), -1, jnp.int32), segment_ids])
    segs_ext = lax.dynamic_slice_in_dim(padded_ids, seq_pos * length, length + CONV - 1)
    segs = segs_ext[CONV - 1 :]
    spans = segs.reshape(span_count, SPAN)
    before = jnp.concatenate([segs_ext[CONV - 2 : CONV - 1], spans[:-1, -1]])
    marks = jnp.stack(
        [(segs_ext[tap : tap + length] == segs).astype(F32) for tap in range(CONV - 1)]
        + [
            (segs == segs_ext[CONV - 2]).astype(F32),
            (spans == before[:, None]).astype(F32).reshape(length),
            (spans == spans[:, -1:]).astype(F32).reshape(length),
            segs.astype(F32),
            jnp.zeros((length,), F32),
        ],
        axis=1,
    )
    seg_rows = segs.astype(F32).reshape(span_count, 1, SPAN)

    def local_cols(values):
        mine = lax.dynamic_slice_in_dim(values, col_start, local_width, values.ndim - 1)
        return jnp.concatenate([mine, values[..., inner_width:]], axis=-1)

    taps = jnp.concatenate(
        [
            local_cols(conv_weight),
            local_cols(conv_bias)[None, :],
            jnp.zeros((3, channels), F32),
        ],
        axis=0,
    )
    pad_heads = (0, LANES - head_count)
    dt_local = jnp.pad(lax.dynamic_slice_in_dim(dt_bias, head_start, head_count), pad_heads)
    rates_local = jnp.pad(
        -jnp.exp(lax.dynamic_slice_in_dim(decay_log, head_start, head_count)), pad_heads
    )
    lane_on = jnp.arange(LANES) < head_count
    raw_dt = raw_s[:, pair_width:] + dt_local[None, :]
    step_sizes = jnp.where(lane_on[None, :], jax.nn.softplus(raw_dt), 0.0)
    heads = jnp.concatenate(
        [dt_local[None, :], rates_local[None, :], jnp.zeros((6, LANES), F32)], axis=0
    )
    head_dim = local_width // head_count
    spread_f = (
        jnp.arange(LANES)[:, None] == (jnp.arange(local_width) // head_dim)[None, :]
    ).astype(F32)
    spread = spread_f.astype(BF16)

    raw_x, low_0, near_0, got_far[0] = lax.optimization_barrier(
        (raw_x, low_0, near_0, got_far[0])
    )
    if middle < experts_half:
        got_far.append(swap(after(sent[middle:], raw_x), SEQ, far_z))
    low_far = [swap(got_far[0], SEQ, 1)]
    route_cols = split_rows(gate_weights)
    route_cols = jnp.concatenate([routes.astype(BF16)] + route_cols, axis=1)
    route_cols = jnp.pad(route_cols, ((0, 0), (0, LANES - route_cols.shape[1])))
    cot_one = jnp.concatenate([cotangent, route_cols], axis=1)

    def tile(cols, turn=lambda i: i):
        return pl.BlockSpec((SPAN, cols), lambda i: (turn(i), 0))

    def whole(*shape):
        return pl.BlockSpec(shape, lambda i: (0,) * len(shape))

    def seg_tile(turn=lambda i: i):
        return pl.BlockSpec((1, 1, SPAN), lambda i: (turn(i), 0, 0))

    shape = jax.ShapeDtypeStruct
    elements = length * SPAN * head_count
    scan_cost = cost(
        4 * elements * LANES, length * (channels * 8 + local_width * 8 + 4096), elements
    )
    conv_out, inputs, bc_low, local_y, reach, entries, last_state = pl.pallas_call(
        scan_forward,
        grid=(span_count,),
        in_specs=[
            tile(local_width),
            tile(raw_s.shape[1]),
            whole(8, channels),
            tile(8),
            seg_tile(),
            whole(8, channels),
            tile(LANES),
            whole(8, LANES),
            whole(LANES, local_width),
        ],
        out_specs=[
            tile(channels),
            tile(local_width),
            tile(pair_width),
            tile(local_width),
            tile(LANES),
            pl.BlockSpec((1, state_dim, local_width), lambda i: (i, 0, 0)),
            whole(state_dim, local_width),
        ],
        out_shape=[
            shape((length, channels), F32),
            shape((length, local_width), BF16),
            shape((length, pair_width), BF16),
            shape((length, local_width), F32),
            shape((length, LANES), F32),
            shape((span_count, state_dim, local_width), F32),
            shape((state_dim, local_width), F32),
        ],
        scratch_shapes=[
            pltpu.VMEM((SPAN + 8, channels), F32),
            pltpu.VMEM((state_dim, local_width), F32),
            pltpu.VMEM((8, LANES), F32),
        ],
        compiler_params=compiler_params(),
        cost_estimate=scan_cost,
        name="scan_forward",
    )(raw_x, raw_s, halo, marks, seg_rows, taps, step_sizes, heads, spread)

    last_state, got_far, low_far[0] = lax.optimization_barrier(
        (last_state, got_far, low_far[0])
    )
    got_far = [after(part, last_state) for part in got_far]
    cot_far = swap(after(cot_one, last_state), SEQ, far_z)
    low_near = swap(after(near_0, last_state), SEQ, 1)
    low_far_rest = got_far[1:]
    got_far = jnp.concatenate(got_far, axis=0)
    near_far = swap(got_far, SEQ, low_z)
    through = jnp.dot(reach[length - 1 :], spread_f, precision=HIGH)
    block_states, block_decays = gather_states(through, last_state)
    state_in = earlier_states(block_states, block_decays)
    local_y, state_in, cot_far, near_far, low_near = lax.optimization_barrier(
        (local_y, state_in, cot_far, near_far, low_near)
    )
    low_far = low_far + [swap(after(part, local_y), SEQ, 1) for part in low_far_rest]
    weight_z, weight_out = both[:, :local_width], both[:, local_width:]
    gate_z = low_dot(in_low, weight_z)
    skip_wide = jnp.dot(
        jnp.pad(lax.dynamic_slice_in_dim(skip_gain, head_start, head_count), pad_heads)[None, :],
        spread_f,
        precision=HIGH,
    )
    gain_local = lax.dynamic_slice_in_dim(gated_gain, col_start, local_width)
    rows_wide = jnp.concatenate(
        [skip_wide, gain_local[None, :], jnp.zeros((6, local_width), F32)], axis=0
    )
    full_y, scaled_low, mixer_part, squares = pl.pallas_call(
        gate_forward,
        grid=(span_count,),
        in_specs=[
            tile(local_width),
            tile(LANES),
            tile(pair_width),
            whole(state_dim, local_width),
            tile(local_width),
            tile(local_width),
            whole(8, local_width),
            whole(LANES, local_width),
            whole(model_width, local_width),
        ],
        out_specs=[tile(local_width), tile(local_width), tile(model_width), tile(1)],
        out_shape=[
            shape((length, local_width), F32),
            shape((length, local_width), BF16),
            shape((length, model_width), BF16),
            shape((length, 1), F32),
        ],
        compiler_params=compiler_params(),
        cost_estimate=cost(
            2 * length * local_width * (model_width + 3 * LANES),
            length * (local_width * 16 + model_width * 2),
        ),
        name="gate_forward",
    )(local_y, reach, bc_low, state_in, inputs, gate_z, rows_wide, spread, weight_out)

    mixer_rows = scatter_exp(mixer_part.reshape(exp_count, rows_here, model_width), exp_strides)
    square_rows = scatter_exp(squares.reshape(exp_count, 1, rows_here), exp_strides)
    square_rows = square_rows.reshape(rows_here, 1)
    scale_mix = lax.rsqrt(square_rows / inner_width + EPS)
    residual = (
        lax.dynamic_slice_in_dim(tokens, exp_pos * rows_here, rows_here).astype(F32)
        + scale_mix * mixer_rows
    )
    scale_mid = rms_scale(residual)
    normed_mid = residual * scale_mid
    mid_low = (normed_mid * norm_mid[None, :]).astype(BF16)
    known = {0: after(cot_one, mixer_rows), exp_count: cot_far}
    for stride in exp_strides[:-1]:
        keys = list(known)
        far = swap(jnp.concatenate([known[at] for at in keys], axis=0), "exp", stride)
        for number, at in enumerate(keys):
            known[at | stride] = far[number * rows_here : (number + 1) * rows_here]
    mid_low, known, *low_far = lax.optimization_barrier((mid_low, known, *low_far))
    mid_all = lax.all_gather(mid_low, GROUP, axis=0, tiled=True)
    low_far_near = swap(near_far, SEQ, 1)
    low_far = jnp.concatenate(low_far, axis=0)
    keys = list(known)
    far = swap(jnp.concatenate([known[at] for at in keys], axis=0), "exp", 1)
    for number, at in enumerate(keys):
        known[at | 1] = far[number * rows_here : (number + 1) * rows_here]
    cot_all = jnp.concatenate([known[at] for at in range(block_count)], axis=0)

    def natural(values):
        return jnp.stack(
            [
                lax.dynamic_index_in_dim(values, at ^ group_pos, 0, False)
                for at in range(block_count)
            ]
        )

    capacity = 2 * rows_here * top_count // (experts_here * exp_count)
    first_expert = exp_pos * experts_here + far_bit * experts_half
    expert_ids = first_expert + jnp.arange(experts_half, dtype=jnp.int32)
    tables = cot_all[:, model_width:].reshape(block_count, rows_here, LANES)
    tables = natural(tables).astype(F32).transpose(0, 2, 1)
    routes_all = tables[:, :top_count].astype(jnp.int32)
    gates_all = sum(
        tables[:, at * top_count : (at + 1) * top_count] for at in range(1, 4)
    )
    named = routes_all[:, :, None, :] == expert_ids[None, None, :, None]
    hit = jnp.any(named, axis=1)
    gate_rows = jnp.sum(jnp.where(named, gates_all[:, :, None, :], 0.0), axis=1)
    order = jnp.triu(jnp.ones((rows_here, rows_here), BF16))
    rank = jnp.einsum("bes,st->bet", hit.astype(BF16), order, preferred_element_type=F32)
    places = jnp.where(hit, rank - 1.0, -1.0)
    place_rows = places.astype(jnp.int32)
    place_cols = places.transpose(0, 2, 1).astype(BF16)
    gate_cols = gate_rows.transpose(0, 2, 1).astype(BF16)
    group_here = jnp.reshape(group_pos, (1,)).astype(jnp.int32)
    grad_got = dispatch(
        cot_all, place_rows, capacity, model_width, gate_rows, group_here
    )
    cot_rows = cot_all[:, :model_width]
    grad_shid = dot_nt(cot_rows, shared_back).reshape(block_count, rows_here, hidden_part)
    grad_shid = natural(grad_shid).reshape(-1, hidden_part)
    sets = {
        0: kept,
        1: low_0,
        low_z: near_0,
        1 | low_z: low_near,
        far_z: got_far,
        1 | far_z: low_far,
        far_z | low_z: near_far,
        1 | far_z | low_z: low_far_near,
    }
    for stride in y_strides[1:]:
        sets.update({at | stride: swap(v, SEQ, stride) for at, v in sets.items()})
    mid_all, grad_got, grad_shid, *sets = lax.optimization_barrier(
        (mid_all, grad_got, grad_shid, *[sets[at] for at in range(seq_count)])
    )

    got = dispatch(mid_all, place_rows, capacity, model_width)
    place_here = jnp.reshape(seq_pos, (1,)).astype(jnp.int32)
    expert_hid, expert_back, expert_res, grad_rows = run_experts(place_here, got, grad_got, sets)
    shared_ab = low_dot(mid_all, shared_in)
    shared_a, shared_b = shared_ab[:, :hidden_part], shared_ab[:, hidden_part:]
    shared_hid = (jax.nn.silu(shared_a) * shared_b).astype(BF16)
    grad_ab = jnp.concatenate(
        [grad_shid * shared_b * silu_slope(shared_a), grad_shid * jax.nn.silu(shared_a)], axis=1
    ).astype(BF16)
    row_part = combine(grad_rows, place_cols, grad_ab, shared_in, True)
    grad_mid = lax.psum_scatter(row_part, GROUP, scatter_dimension=0, tiled=True)
    known = dict(
        enumerate(
            expert_grads(
                place_here, got, grad_got, after(expert_hid, row_part), expert_back, seq_count
            )
        )
    )

    def reduced(at, stride, *wait):
        sent = after(known[at | stride], *wait) if wait else known[at | stride]
        known[at] = added(known[at], swap(sent, SEQ, stride))
        return known[at]

    for stride in reversed(y_strides[1:]):
        for at in [at for at in known if at & stride]:
            reduced(at ^ stride, stride)
            del known[at]
    grad_ab = after(grad_ab, known[0])
    shared_grads = jnp.concatenate(
        [
            dot_tn(grad_ab, mid_all),
            dot_tn(
                natural(shared_hid.reshape(block_count, rows_here, -1)).reshape(
                    shared_hid.shape
                ),
                cot_rows,
            ),
        ],
        axis=0,
    ).astype(BF16)
    first_sum = reduced(low_z | far_z, 1)
    grad_mid, shared_grads = lax.optimization_barrier((grad_mid, shared_grads))
    grad_mid = grad_mid.astype(F32)
    second_sum = reduced(far_z, 1)
    shard = lax.psum_scatter(
        shared_grads, ("near", "low"), scatter_dimension=0, tiled=True
    )
    pieces = lax.all_gather(shard, ALL, axis=0, tiled=True)

    grad_norm_mid = jnp.sum(grad_mid * normed_mid, axis=0)
    grad_resid = cotangent.astype(F32) + norm_back(grad_mid, norm_mid, normed_mid, scale_mid)
    grad_part = (scale_mix * grad_resid).astype(BF16)
    grad_square = (
        jnp.sum(grad_resid * mixer_rows, axis=1, keepdims=True) * -0.5 * scale_mix**3 / inner_width
    ).astype(BF16)
    grad_part_all = gather_exp(grad_part, exp_strides)
    grad_square_all = gather_exp(grad_square.reshape(1, rows_here), exp_strides)
    grad_square_all = grad_square_all.astype(F32).reshape(length, 1)

    grad_part_all, known[far_z], known[low_z | far_z], expert_res = lax.optimization_barrier(
        (grad_part_all, known[far_z], known[low_z | far_z], expert_res)
    )
    out_part = combine(
        expert_res, place_cols, shared_hid, shared_back, False, gate_cols
    )
    third_sum = reduced(far_z, low_z)

    grad_y, grad_z, gate_sums, direct = pl.pallas_call(
        gate_backward,
        grid=(span_count,),
        in_specs=[
            tile(model_width),
            tile(1),
            tile(local_width),
            tile(local_width),
            tile(local_width),
            tile(LANES),
            tile(pair_width),
            whole(8, local_width),
            whole(LANES, local_width),
            whole(model_width, local_width),
        ],
        out_specs=[
            tile(local_width),
            tile(local_width),
            whole(8, local_width),
            whole(state_dim, local_width),
        ],
        out_shape=[
            shape((length, local_width), BF16),
            shape((length, local_width), BF16),
            shape((8, local_width), F32),
            shape((state_dim, local_width), F32),
        ],
        compiler_params=compiler_params(),
        cost_estimate=cost(
            2 * length * local_width * (model_width + 3 * LANES),
            length * (local_width * 16 + model_width * 2),
        ),
        name="gate_backward",
    )(
        grad_part_all,
        grad_square_all,
        full_y,
        gate_z,
        inputs,
        reach,
        bc_low,
        rows_wide,
        spread,
        weight_out,
    )
    fourth_sum = reduced(low_z, 1)
    state_grad = later_grads(
        lax.all_gather(direct.astype(BF16), SEQ, axis=0).astype(F32), block_decays
    )

    small_first = y_strides + [low_z, far_z]
    sent = jnp.concatenate([dot_tn(in_low, grad_z), dot_tn(grad_part_all, scaled_low)], axis=1)
    sent, third_sum, fourth_sum, known[1] = lax.optimization_barrier(
        (sent.astype(BF16), third_sum, fourth_sum, known[1])
    )
    far_back = [swap(third_sum[:middle], SEQ, far_z)]
    low_sent = swap(known[1], SEQ, 1)
    sent, sent_left = scatter_step(sent, small_first[0], None)
    grad_y, state_grad, out_part, sent = lax.optimization_barrier(
        (grad_y, state_grad, out_part, sent)
    )
    near_sent = swap(fourth_sum, SEQ, low_z)
    routed = lax.psum_scatter(out_part, GROUP, scatter_dimension=0, tiled=True).astype(F32)
    passed = jnp.concatenate([jnp.ones((1, LANES), F32), reach[SPAN - 1 : length - 1 : SPAN]])
    passed = jnp.broadcast_to(passed[:, None, :], (span_count, 8, LANES))
    turn = lambda i: span_count - 1 - i
    ahead = SPAN // 8
    before_tile = lambda cols: pl.BlockSpec(
        (8, cols), lambda i: (jnp.maximum(turn(i) * ahead - 1, 0), 0)
    )
    grad_x, grad_bc, grad_steps, tail_rows, head_rows, conv_sums, rate_sums = pl.pallas_call(
        scan_backward,
        grid=(span_count,),
        in_specs=[
            tile(channels, turn),
            tile(local_width, turn),
            tile(raw_s.shape[1], turn),
            before_tile(local_width),
            before_tile(raw_s.shape[1]),
            whole(8, channels),
            tile(8, turn),
            seg_tile(turn),
            whole(8, channels),
            tile(LANES, turn),
            whole(8, LANES),
            whole(LANES, local_width),
            whole(local_width, LANES),
            tile(local_width, turn),
            tile(pair_width, turn),
            tile(local_width, turn),
            tile(local_width, turn),
            pl.BlockSpec((1, state_dim, local_width), lambda i: (turn(i), 0, 0)),
            pl.BlockSpec((1, 8, LANES), lambda i: (turn(i), 0, 0)),
            whole(state_dim, local_width),
            whole(state_dim, local_width),
            whole(8, local_width),
        ],
        out_specs=[
            tile(local_width, turn),
            tile(pair_width, turn),
            tile(LANES, turn),
            whole(8, channels),
            whole(8, channels),
            whole(8, channels),
            whole(8, LANES),
        ],
        out_shape=[
            shape((length, local_width), BF16),
            shape((length, pair_width), BF16),
            shape((length, LANES), F32),
            shape((8, channels), F32),
            shape((8, channels), F32),
            shape((8, channels), F32),
            shape((8, LANES), F32),
        ],
        scratch_shapes=[pltpu.VMEM((SPAN + 8, channels), F32)] * 4
        + [pltpu.VMEM((state_dim, local_width), F32), pltpu.VMEM((local_width, SPAN), F32)],
        compiler_params=compiler_params(),
        cost_estimate=cost(
            10 * elements * LANES, length * (channels * 16 + local_width * 16 + 4096), elements
        ),
        name="scan_backward",
    )(
        conv_out,
        raw_x,
        raw_s,
        raw_x,
        raw_s,
        halo,
        marks,
        seg_rows,
        taps,
        step_sizes,
        heads,
        spread,
        spread.T,
        inputs,
        bc_low,
        full_y,
        grad_y,
        entries,
        passed,
        state_in,
        state_grad,
        rows_wide,
    )
    (
        grad_x,
        grad_bc,
        grad_steps,
        tail_rows,
        head_rows,
        conv_sums,
        rate_sums,
        far_back[0],
        third_sum,
        low_sent,
        near_sent,
    ) = lax.optimization_barrier(
        (
            grad_x,
            grad_bc,
            grad_steps,
            tail_rows,
            head_rows,
            conv_sums,
            rate_sums,
            far_back[0],
            third_sum,
            low_sent,
            near_sent,
        )
    )
    if middle < experts_half:
        far_back.append(swap(third_sum[middle:], SEQ, far_z))
    edge = jnp.stack(
        [
            sum(
                taps[tap] * marks[at - tap, tap] * head_rows[at - tap]
                for tap in range(at + 1)
            )
            for at in range(CONV - 1)
        ]
    )
    block_output = (residual + routed).astype(BF16)

    edge = jnp.pad(edge, ((8 - (CONV - 1), 0), (0, 0))).astype(BF16)
    edge_x, edge_bc = edge[:, :local_width], edge[:, local_width:]
    grad_dt_raw = grad_steps * jax.nn.sigmoid(raw_dt) * lane_on.astype(F32)[None, :]
    grad_dt = grad_dt_raw.astype(BF16)
    grad_late = jnp.concatenate(
        [
            dot_tn(in_low, grad_x) + dot_tn(halo_low, edge_x),
            dot_tn(in_low, grad_dt),
            dot_tn(in_low, grad_bc) + dot_tn(halo_low, edge_bc),
        ],
        axis=1,
    ).astype(BF16)
    late_sum, late_left = scatter_step(grad_late, small_first[0], None)
    grad_x, late_sum, sent, far_back = lax.optimization_barrier(
        (grad_x, late_sum, sent, far_back)
    )
    for stride in small_first[1:]:
        sent, sent_left = scatter_step(sent, stride, sent_left)
    sent = sent.astype(F32)
    sum_wz, sum_wout = sent[:, :local_width], sent[:, local_width:].T
    last_sum = added(added(known[0], low_sent), near_sent)
    owned = owner_grads(
        jnp.reshape(far_bit, (1,)).astype(jnp.int32),
        [last_sum, jnp.concatenate(far_back, axis=0)],
    )
    grad_in = (
        dot_nt(grad_z, weight_z)
        + dot_nt(grad_x, weight_x)
        + dot_nt(grad_dt, weight_dt)
        + dot_nt(grad_bc, proj_bc)
    )
    for stride in small_first[1:]:
        late_sum, late_left = scatter_step(late_sum, stride, late_left)
        if stride == low_z:
            late_sum, owned = lax.optimization_barrier((late_sum, owned))
    sum_gate_e, sum_up_e, sum_down_e = owned
    late_sum, conv_sums, rate_sums, gate_sums, grad_norm_mid = lax.optimization_barrier(
        (late_sum, conv_sums, rate_sums, gate_sums, grad_norm_mid)
    )
    late_sum = late_sum.astype(F32)
    sum_wxdt = late_sum[:, : local_width + LANES]
    sum_wbc = sum_all(late_sum[:, local_width + LANES :], "exp", exp_strides).astype(BF16)
    for stride in seq_strides:
        other = swap(sum_wbc, SEQ, stride)
        low = bit_of(SEQ, stride) == 0
        sum_wbc = jnp.where(
            low,
            jnp.concatenate([sum_wbc, other], axis=0),
            jnp.concatenate([other, sum_wbc], axis=0),
        )
    normed_in = tokens_f * scale_in
    halo_scale = rms_scale(halo_f)
    halo_normed = halo_f * halo_scale
    edge_in = dot_nt(edge_x, weight_x) + dot_nt(edge_bc, proj_bc)
    grad_norm_in = jnp.sum(grad_in * normed_in, axis=0) + jnp.sum(edge_in * halo_normed, axis=0)
    edge_part = lax.ppermute(
        norm_back(edge_in, norm_in, halo_normed, halo_scale),
        SEQ,
        [(i + 1, i) for i in range(seq_count - 1)],
    )
    grad_in_part = norm_back(grad_in, norm_in, normed_in, scale_in).astype(BF16)
    grad_in_part = grad_in_part.at[length - 8 :].set(
        (grad_in_part[length - 8 :].astype(F32) + edge_part).astype(BF16)
    )
    tokens_grad = grad_resid + scatter_exp(
        grad_in_part.reshape(exp_count, rows_here, model_width), exp_strides
    )

    pieces = pieces.reshape(
        2, 2, low_z, exp_count, shard.shape[0], model_width
    ).transpose(0, 3, 1, 2, 4, 5)
    pieces = pieces.reshape(block_count, 3, hidden_part, model_width).transpose(1, 0, 2, 3)
    pieces = pieces.reshape(3, block_count * hidden_part, model_width)

    def rows_of(values):
        flat = values.reshape(-1)
        count = -(-flat.shape[0] // local_width)
        return jnp.pad(flat, (0, count * local_width - flat.shape[0])).reshape(count, local_width)

    skip_sums = jnp.dot(gate_sums[1:2], spread_f.T, precision=HIGH)
    head_rows3 = jnp.concatenate(
        [jnp.sum(grad_dt_raw, axis=0, keepdims=True), rate_sums[:1] * rates_local, skip_sums]
    )
    own_sums = jnp.concatenate(
        [
            conv_sums[: CONV + 1, :local_width],
            gate_sums[:1],
            jnp.pad(head_rows3, ((0, 0), (0, local_width - LANES))),
        ]
    )
    shared_sums = jnp.concatenate(
        [rows_of(conv_sums[: CONV + 1, local_width:]), rows_of(grad_norm_mid)]
    )
    own_count = own_sums.shape[0]
    all_sums = sum_all(jnp.concatenate([own_sums, shared_sums]), SEQ, seq_strides)
    shared_sums = sum_all(all_sums[own_count:], "exp", exp_strides).reshape(-1)
    own_all = gather_exp(all_sums[None, :own_count], exp_strides)
    sum_norm_in = sum_all(
        sum_all(rows_of(grad_norm_in), SEQ, seq_strides), "exp", exp_strides
    ).reshape(-1)[:model_width]
    wide = own_all.transpose(1, 0, 2).reshape(own_count, inner_width)
    head_sums = own_all[:, CONV + 2 :, :head_count].transpose(1, 0, 2).reshape(3, head_total)
    pair_count = (CONV + 1) * pair_width
    pair_sums = shared_sums[:pair_count].reshape(CONV + 1, pair_width)
    pair_rows = -(-pair_count // local_width) * local_width
    conv_all = jnp.concatenate([wide[: CONV + 1], pair_sums], axis=1)
    return (
        block_output,
        tokens_grad,
        sum_norm_in,
        sum_wz,
        sum_wxdt[:, :local_width],
        sum_wbc.astype(F32),
        sum_wxdt[:, local_width : local_width + head_count],
        conv_all[:CONV],
        conv_all[CONV],
        head_sums[0],
        head_sums[1],
        head_sums[2],
        wide[CONV + 1],
        sum_wout,
        shared_sums[pair_rows : pair_rows + model_width],
        sum_gate_e,
        sum_up_e,
        sum_down_e,
        pieces[0].T.astype(F32),
        pieces[1].T.astype(F32),
        pieces[2].astype(F32),
    )


def solution(mesh):
    placed = (
        P(SEQ, None),
        P(),
        P(ALL, None),
        P(ALL, None),
        P(ALL, None),
        P(),
        P(SEQ, "exp"),
        P(SEQ, "exp"),
        P(),
        P(SEQ, "exp"),
        P(),
        P(),
        P(),
        P(),
        P(),
        P(),
        P("exp", SEQ),
        P(),
        P("exp", SEQ, None),
        P("exp", SEQ, None),
        P("exp", None, SEQ),
        P(),
        P(),
        P(),
    )
    seq_count, exp_count = mesh.devices.shape
    split = Mesh(
        mesh.devices.reshape(2, 2, seq_count // 4, exp_count), ("far", "near", "low", "exp")
    )
    return jax.shard_map(
        per_device,
        mesh=split,
        in_specs=placed,
        out_specs=(
            P(ALL, None),
            P(ALL, None),
            P(),
            P(SEQ, "exp"),
            P(SEQ, "exp"),
            P(),
            P(SEQ, "exp"),
            P(),
            P(),
            P(),
            P(),
            P(),
            P(),
            P("exp", SEQ),
            P(),
            P("exp", SEQ, None),
            P("exp", SEQ, None),
            P("exp", None, SEQ),
            P(),
            P(),
            P(),
        ),
        check_vma=False,
    )
```

```python
from functools import partial

import jax
import jax.numpy as jnp
from jax import lax
from jax.experimental import pallas as pl
from jax.experimental.pallas import tpu as pltpu
from jax.sharding import Mesh
from jax.sharding import PartitionSpec as P

CONV = 4
SPAN = 256
LANES = 128
EPS = 1e-05
FLOOR = -1e30
HIGH = lax.Precision.HIGHEST
SEQ = ("far", "near", "low")
GROUP = ("far", "exp")
ALL = SEQ + ("exp",)
VMEM_BYTES = 56 * 1024 * 1024
F32 = jnp.float32
BF16 = jnp.bfloat16


def low_dot(left, right):
    return jnp.dot(left, right, preferred_element_type=F32)


def dot_nt(left, right):
    return lax.dot_general(left, right, (((1,), (1,)), ((), ())), preferred_element_type=F32)


def dot_tn(left, right):
    return lax.dot_general(left, right, (((0,), (0,)), ((), ())), preferred_element_type=F32)


def split_dot(values, table):
    high = values.astype(BF16)
    rest = (values - high.astype(F32)).astype(BF16)
    return low_dot(high, table) + low_dot(rest, table)


def exact_sum(triangle, values):
    high = values.astype(BF16)
    rest = values - high.astype(F32)
    middle = rest.astype(BF16)
    small = (rest - middle.astype(F32)).astype(BF16)
    return low_dot(triangle, high) + low_dot(triangle, middle) + low_dot(triangle, small)


def silu_slope(values):
    sigmoid_v = jax.nn.sigmoid(values)
    return sigmoid_v * (1.0 + values * (1.0 - sigmoid_v))


def rms_scale(values):
    return lax.rsqrt(jnp.mean(values * values, axis=-1, keepdims=True) + EPS)


def norm_back(grad_normed, gain, normed, scale):
    weighted = grad_normed * gain[None, :]
    return scale * (weighted - normed * jnp.mean(weighted * normed, axis=-1, keepdims=True))


def compiler_params(steps=1):
    return pltpu.CompilerParams(
        dimension_semantics=("arbitrary",) * steps, vmem_limit_bytes=VMEM_BYTES
    )


def cost(flops, moved, exps=0):
    return pl.CostEstimate(flops=int(flops), bytes_accessed=int(moved), transcendentals=int(exps))


def causal(span):
    rows = lax.broadcasted_iota(jnp.int32, (span, span), 0)
    cols = lax.broadcasted_iota(jnp.int32, (span, span), 1)
    return rows >= cols


def span_terms(steps, marks, seg_row, rates, b_low, c_low):
    span = steps.shape[0]
    keep = causal(span)
    cum = exact_sum(keep.astype(F32).astype(BF16), steps * rates)
    cum_rows = cum.T
    same = marks[:, 6:7] == seg_row
    bias = jnp.where(keep & same, 0.0, FLOOR)
    scores = dot_nt(c_low, b_low)
    last = cum[span - 1 : span, :]
    entry = jnp.exp(cum) * marks[:, 4:5]
    tail = jnp.exp(last - cum) * marks[:, 5:6]
    return cum, cum_rows, bias, scores, last, entry, tail


def scan_forward(
    raw_x,
    raw_s,
    halo,
    marks,
    seg_row,
    taps,
    steps,
    heads,
    spread,
    conv_out,
    x_out,
    bc_out,
    y_out,
    reach_out,
    entries_out,
    last_out,
    ext,
    state,
    total,
):
    turn = pl.program_id(0)
    span, width = raw_x.shape
    channels = taps.shape[1]

    @pl.when(turn == 0)
    def _():
        ext[0:8, :] = halo[...]
        state[...] = jnp.zeros_like(state)
        total[...] = jnp.zeros_like(total)

    @pl.when(turn > 0)
    def _():
        ext[0:8, :] = ext[span : span + 8, :]

    ext[8 : 8 + span, 0:width] = raw_x[...]
    ext[8 : 8 + span, width:channels] = raw_s[:, 0 : channels - width]
    mark = marks[...]
    for start in range(0, channels, LANES):
        cols = slice(start, start + LANES)
        conv = taps[4:5, cols] + taps[3:4, cols] * ext[8 : 8 + span, cols]
        for tap in range(CONV - 1):
            conv = conv + taps[tap : tap + 1, cols] * (
                ext[5 + tap : 5 + tap + span, cols] * mark[:, tap : tap + 1]
            )
        conv_out[:, cols] = conv
        act = (conv * jax.nn.sigmoid(conv)).astype(BF16)
        if start < width:
            x_out[:, cols] = act
        else:
            bc_out[:, start - width : start - width + LANES] = act
    half = (channels - width) // 2
    b_low = bc_out[:, 0:half]
    c_low = bc_out[:, half:]
    step = steps[...]
    rates = heads[1:2, :]
    cum, cum_rows, bias, scores, last, entry, tail = span_terms(
        step, mark, seg_row[0], rates, b_low, c_low
    )
    reach_out[...] = jnp.exp(cum + total[0:1, :]) * mark[:, 3:4]
    total[0:1, :] = total[0:1, :] + last
    table = spread[...]
    entry_wide = split_dot(entry, table)
    xf = x_out[...].astype(F32)
    fed = (xf * split_dot(step, table)).astype(BF16)
    kept = (xf * split_dot(tail * step, table)).astype(BF16)
    entries_out[0] = state[...]
    state_low = state[...].astype(BF16)
    y_out[...] = entry_wide * low_dot(c_low, state_low)
    left_half = lax.broadcasted_iota(jnp.int32, (span, LANES), 1) < LANES // 2
    for pair in range(width // LANES):
        cols = slice(pair * LANES, (pair + 1) * LANES)
        both = []
        for head in (2 * pair, 2 * pair + 1):
            decay = jnp.exp(cum[:, head : head + 1] - cum_rows[head : head + 1, :] + bias)
            both.append(low_dot((decay * scores).astype(BF16), fed[:, cols]))
        y_out[:, cols] = y_out[:, cols] + jnp.where(left_half, both[0], both[1])
    state[...] = state[...] * entry_wide[span - 1 : span, :] + dot_tn(b_low, kept)

    @pl.when(turn == pl.num_programs(0) - 1)
    def _():
        last_out[...] = state[...]


def gate_forward(
    y_local,
    reach,
    bc,
    state_in,
    x,
    gate,
    rows,
    spread,
    weight,
    full_out,
    low_out,
    mixer_out,
    square_out,
):
    half = bc.shape[1] // 2
    c_low = bc[:, half:]
    far = split_dot(reach[...], spread[...]) * low_dot(c_low, state_in[...].astype(BF16))
    full = y_local[...] + far + rows[0:1, :] * x[...].astype(F32)
    full_out[...] = full
    z = gate[...]
    gated = full * (z * jax.nn.sigmoid(z))
    square_out[...] = jnp.sum(gated * gated, axis=1, keepdims=True)
    low = (gated * rows[1:2, :]).astype(BF16)
    low_out[...] = low
    mixer_out[...] = dot_nt(low, weight[...]).astype(BF16)


def gate_backward(
    part_grad,
    square_grad,
    full_y,
    gate,
    x,
    reach,
    bc,
    rows,
    spread,
    weight,
    grad_y_out,
    grad_z_out,
    sums_out,
    direct_out,
):
    turn = pl.program_id(0)
    z = gate[...]
    sig = jax.nn.sigmoid(z)
    act = z * sig
    full = full_y[...]
    gated = full * act
    scaled_grad = low_dot(part_grad[...], weight[...])
    gated_grad = scaled_grad * rows[1:2, :] + 2.0 * gated * square_grad[...]
    grad_full = gated_grad * act
    grad_y_out[...] = grad_full.astype(BF16)
    grad_z_out[...] = (gated_grad * full * (sig * (1.0 + z * (1.0 - sig)))).astype(BF16)
    half = bc.shape[1] // 2
    seen = (grad_full * split_dot(reach[...], spread[...])).astype(BF16)
    direct = dot_tn(bc[:, half:], seen)
    gain_sum = jnp.sum(scaled_grad * gated, axis=0, keepdims=True)
    skip_sum = jnp.sum(grad_full * x[...].astype(F32), axis=0, keepdims=True)

    @pl.when(turn == 0)
    def _():
        sums_out[...] = jnp.zeros_like(sums_out)
        direct_out[...] = jnp.zeros_like(direct_out)

    sums_out[0:1, :] = sums_out[0:1, :] + gain_sum
    sums_out[1:2, :] = sums_out[1:2, :] + skip_sum
    direct_out[...] = direct_out[...] + direct


def scan_backward(
    conv,
    raw_x,
    raw_s,
    raw_x_before,
    raw_s_before,
    halo,
    marks,
    seg_row,
    taps,
    steps,
    heads,
    spread,
    fold,
    x,
    bc,
    full_y,
    grad_y,
    entries,
    passed,
    state_in,
    state_grad,
    rows,
    grad_x_out,
    grad_bc_out,
    grad_step_out,
    tail_out,
    head_out,
    sums_out,
    rates_out,
    ext,
    later0,
    later1,
    later2,
    back,
    turned,
):
    turn = pl.program_id(0)
    span, width = raw_x.shape
    channels = taps.shape[1]
    half = (channels - width) // 2
    later = (later0, later1, later2)

    @pl.when(turn == 0)
    def _():
        back[...] = state_grad[...]
        sums_out[...] = jnp.zeros_like(sums_out)
        rates_out[...] = jnp.zeros_like(rates_out)
        for kept in later:
            kept[span : span + 8, :] = jnp.zeros((8, channels), F32)

    @pl.when(turn > 0)
    def _():
        for kept in later:
            kept[span : span + 8, :] = kept[0:8, :]

    @pl.when(turn == pl.num_programs(0) - 1)
    def _():
        ext[0:8, :] = halo[...]

    @pl.when(turn < pl.num_programs(0) - 1)
    def _():
        ext[0:8, 0:width] = raw_x_before[...]
        ext[0:8, width:channels] = raw_s_before[:, 0 : channels - width]

    ext[8 : 8 + span, 0:width] = raw_x[...]
    ext[8 : 8 + span, width:channels] = raw_s[:, 0 : channels - width]
    mark = marks[...]
    step = steps[...]
    rates = heads[1:2, :]
    b_low = bc[:, 0:half]
    c_low = bc[:, half:]
    cum, cum_rows, bias, scores, last, entry, tail = span_terms(
        step, mark, seg_row[0], rates, b_low, c_low
    )
    table = spread[...]
    entry_wide = split_dot(entry, table)
    tail_wide = split_dot(tail, table)
    step_wide = split_dot(step, table)
    xf = x[...].astype(F32)
    fed_low = (xf * step_wide).astype(BF16)
    fed = fed_low.astype(F32)
    dy_low = grad_y[...]
    dy = dy_low.astype(F32)
    seen = (dy * entry_wide).astype(BF16)
    entered = entries[0] + split_dot(passed[0], table)[0:1, :] * state_in[...]
    entered_low = entered.astype(BF16)
    back_low = back[...].astype(BF16)
    turned_dy = dy.T.astype(BF16)
    left_half = lax.broadcasted_iota(jnp.int32, (span, LANES), 1) < LANES // 2
    score_grad = jnp.zeros((span, span), F32)
    head_rows = LANES // 2
    for pair in range(width // LANES):
        cols = slice(pair * LANES, (pair + 1) * LANES)
        fed_pair = fed_low[:, cols]
        dy_pair = dy[:, cols]
        for side in (0, 1):
            head = 2 * pair + side
            decay = jnp.exp(cum[:, head : head + 1] - cum_rows[head : head + 1, :] + bias)
            weights = (decay * scores).astype(BF16)
            own = jnp.where(left_half if side == 0 else ~left_half, dy_pair, 0.0).astype(BF16)
            score_grad = score_grad + dot_nt(own, fed_pair) * decay
            lanes = slice(head * head_rows, (head + 1) * head_rows)
            turned[lanes, :] = low_dot(turned_dy[lanes, :], weights)
    score_low = score_grad.astype(BF16)
    inner = turned[...].T
    far = tail_wide * low_dot(b_low, back_low)
    fed_grad = inner + far
    skip = rows[0:1, :]
    scan_y = full_y[...] - skip * xf
    summed = fold[...]
    far_sums = split_dot(fed * far, summed)
    kept_row = jnp.sum(back[...] * entered, axis=0, keepdims=True) * entry_wide[span - 1 : span, :]
    kept_sum = split_dot(jnp.broadcast_to(kept_row, (8, width)), summed)[0:1, :]
    log_grad = split_dot(dy * scan_y - fed * fed_grad, summed)
    ends = jnp.sum(far_sums, axis=0, keepdims=True) + kept_sum
    rows_i = lax.broadcasted_iota(jnp.int32, (span, span), 0)
    cols_i = lax.broadcasted_iota(jnp.int32, (span, span), 1)
    upper = (cols_i >= rows_i).astype(F32).astype(BF16)
    rate_step_grad = exact_sum(upper, log_grad) + ends
    grad_step_out[...] = split_dot(fed_grad * xf, summed) + rates * rate_step_grad
    rates_out[0:1, :] = rates_out[0:1, :] + jnp.sum(rate_step_grad * step, axis=0, keepdims=True)
    c_grad = dot_nt(seen, entered_low) + low_dot(score_low, b_low)
    b_grad = dot_nt((fed * tail_wide).astype(BF16), back_low) + dot_tn(score_low, c_low)
    back[...] = back[...] * entry_wide[span - 1 : span, :] + dot_tn(c_low, seen)
    x_grad = fed_grad * step_wide + skip * dy
    for start in range(0, channels, LANES):
        cols = slice(start, start + LANES)
        if start < width:
            active = x_grad[:, cols]
        elif start < width + half:
            active = b_grad
        else:
            active = c_grad
        grad = active * silu_slope(conv[:, cols])

        @pl.when(turn == pl.num_programs(0) - 1)
        def _():
            head_out[:, cols] = grad[0:8, :]

        source = taps[3:4, cols] * grad
        sums_out[4:5, cols] = sums_out[4:5, cols] + jnp.sum(grad, axis=0, keepdims=True)
        sums_out[3:4, cols] = sums_out[3:4, cols] + jnp.sum(
            grad * ext[8 : 8 + span, cols], axis=0, keepdims=True
        )
        for tap in range(CONV - 1):
            masked = grad * mark[:, tap : tap + 1]
            later[tap][0:span, cols] = masked
            sums_out[tap : tap + 1, cols] = sums_out[tap : tap + 1, cols] + jnp.sum(
                masked * ext[5 + tap : 5 + tap + span, cols], axis=0, keepdims=True
            )
            shift = CONV - 1 - tap
            source = source + taps[tap : tap + 1, cols] * later[tap][shift : shift + span, cols]
        if start < width:
            grad_x_out[:, cols] = source.astype(BF16)
        else:
            grad_bc_out[:, start - width : start - width + LANES] = source.astype(BF16)

        @pl.when(turn == 0)
        def _():
            tail_out[:, cols] = source[span - 8 : span, :]


def dispatch_kernel(weighted, *refs):
    if weighted:
        rows, places, gates, out = refs
    else:
        rows, places, out = refs
    experts, _, slots, _ = out.shape
    count = rows.shape[0]
    slot = lax.broadcasted_iota(jnp.int32, (slots, count), 0)
    hits = [slot == places[0, e : e + 1, :] for e in range(experts)]
    chosen = jnp.concatenate([hit.astype(F32).astype(BF16) for hit in hits], axis=0)
    taken = low_dot(chosen, rows[...])
    for e in range(experts):
        part = taken[e * slots : (e + 1) * slots, :]
        if weighted:
            part = part * jnp.sum(
                jnp.where(hits[e], gates[0, e : e + 1, :], 0.0), axis=1, keepdims=True
            )
        out[e, 0] = part.astype(BF16)


def dispatch(rows, places, slots, width, gates=None, here=None):
    blocks, experts, count = places.shape
    arrays = (rows, places) if gates is None else (rows, places, gates)
    kernel = partial(dispatch_kernel, gates is not None)
    here = jnp.zeros((1,), jnp.int32) if here is None else here
    small = pl.BlockSpec((1, experts, count), lambda b, here: (b, 0, 0))
    return pl.pallas_call(
        lambda here, *refs: kernel(*refs),
        grid_spec=pltpu.PrefetchScalarGridSpec(
            num_scalar_prefetch=1,
            grid=(blocks,),
            in_specs=[pl.BlockSpec((count, width), lambda b, here: (b ^ here[0], 0))]
            + [small] * (len(arrays) - 1),
            out_specs=pl.BlockSpec(
                (experts, 1, slots, width), lambda b, here: (0, b, 0, 0)
            ),
        ),
        out_shape=jax.ShapeDtypeStruct((experts, blocks, slots, width), BF16),
        compiler_params=compiler_params(),
        cost_estimate=cost(
            2 * blocks * experts * slots * count * width,
            2 * blocks * count * width + 2 * experts * blocks * slots * width,
        ),
        name="dispatch",
    )(here, *arrays)


def expert_kernel(pieces, me, got, grad_got, *refs):
    weights = refs[:pieces]
    hid_out, grads_out, res_out, row_out, full = refs[pieces:]
    part = weights[0].shape[-2]
    hidden = hid_out.shape[2]
    for piece, ref in enumerate(weights):
        start = pl.multiple_of((me[0] ^ piece) * part, part)
        full[pl.ds(start, part), :] = ref[0]
    gate, up, down = (slice(kind * hidden, (kind + 1) * hidden) for kind in range(3))
    blocks, slots, width = got.shape[1:]
    step = max(1, min(blocks, 384 // slots))
    for first in range(0, blocks, step):
        rows = slice(first * slots, (first + step) * slots)
        taken = got[0, first : first + step].reshape(step * slots, width)
        taken_grad = grad_got[0, first : first + step].reshape(step * slots, width)
        a = low_dot(taken, full[:, gate])
        b = low_dot(taken, full[:, up])
        hid_grad = low_dot(taken_grad, full[:, down])
        sig = jax.nn.sigmoid(a)
        act = a * sig
        hid = (act * b).astype(BF16)
        a_grad = (hid_grad * b * (sig * (1.0 + a * (1.0 - sig)))).astype(BF16)
        b_grad = (hid_grad * act).astype(BF16)
        hid_out[0, rows, :] = hid
        grads_out[0, rows, 0:hidden] = a_grad
        grads_out[0, rows, hidden:] = b_grad
        res = dot_nt(hid, full[:, down]).astype(BF16)
        row = (dot_nt(a_grad, full[:, gate]) + dot_nt(b_grad, full[:, up])).astype(BF16)
        res_out[0, first : first + step] = res.reshape(step, slots, width)
        row_out[0, first : first + step] = row.reshape(step, slots, width)


def run_experts(me, got, grad_got, pieces):
    count, blocks, slots, width = got.shape
    part, packed = pieces[0].shape[1:]
    hidden = packed // 3
    total = blocks * slots
    wide = pl.BlockSpec((1, blocks, slots, width), lambda e, me: (e, 0, 0, 0))
    narrow = pl.BlockSpec((1, total, hidden), lambda e, me: (e, 0, 0))
    double = pl.BlockSpec((1, total, 2 * hidden), lambda e, me: (e, 0, 0))
    piece = pl.BlockSpec((1, part, packed), lambda e, me: (e, 0, 0))
    shape = jax.ShapeDtypeStruct
    row_shape = shape((count, blocks, slots, width), BF16)
    return pl.pallas_call(
        partial(expert_kernel, len(pieces)),
        grid_spec=pltpu.PrefetchScalarGridSpec(
            num_scalar_prefetch=1,
            grid=(count,),
            in_specs=[wide, wide] + [piece] * len(pieces),
            out_specs=[narrow, double, wide, wide],
            scratch_shapes=[pltpu.VMEM((width, packed), BF16)],
        ),
        out_shape=[
            shape((count, total, hidden), BF16),
            shape((count, total, 2 * hidden), BF16),
            row_shape,
            row_shape,
        ],
        compiler_params=compiler_params(),
        cost_estimate=cost(
            12 * count * total * width * hidden,
            count * (8 * total * width + 6 * width * hidden),
            count * total * hidden,
        ),
        name="experts",
    )(me, got, grad_got, *pieces)


def expert_grad_kernel(pieces, me, got, grad_got, hid, grads, *refs):
    outs, full = refs[:pieces], refs[pieces]
    blocks, slots, width = got.shape[1:]
    part = outs[0].shape[1]
    hidden = hid.shape[2]
    total = blocks * slots
    step = 256
    for start in range(0, width, step):
        cols = slice(start, start + step)
        taken = got[0, :, :, cols].reshape(total, step)
        taken_grad = grad_got[0, :, :, cols].reshape(total, step)
        full[cols, 0 : 2 * hidden] = dot_tn(taken, grads[0]).astype(BF16)
        full[cols, 2 * hidden :] = dot_tn(taken_grad, hid[0]).astype(BF16)
    for piece in range(pieces):
        start = pl.multiple_of((me[0] ^ piece) * part, part)
        outs[piece][0] = full[pl.ds(start, part), :]


def expert_grads(me, got, grad_got, hid, grads, pieces):
    count, blocks, slots, width = got.shape
    total, hidden = hid.shape[1:]
    part = width // pieces
    packed = 3 * hidden
    wide = pl.BlockSpec((1, blocks, slots, width), lambda e, me: (e, 0, 0, 0))
    narrow = pl.BlockSpec((1, total, hidden), lambda e, me: (e, 0, 0))
    double = pl.BlockSpec((1, total, 2 * hidden), lambda e, me: (e, 0, 0))
    piece = pl.BlockSpec((1, part, packed), lambda e, me: (e, 0, 0))
    return pl.pallas_call(
        partial(expert_grad_kernel, pieces),
        grid_spec=pltpu.PrefetchScalarGridSpec(
            num_scalar_prefetch=1,
            grid=(count,),
            in_specs=[wide] * 2 + [narrow, double],
            out_specs=[piece] * pieces,
            scratch_shapes=[pltpu.VMEM((width, packed), BF16)],
        ),
        out_shape=[jax.ShapeDtypeStruct((count, part, packed), BF16)] * pieces,
        compiler_params=compiler_params(),
        cost_estimate=cost(
            6 * count * total * width * hidden, count * (4 * total * width + 6 * width * hidden)
        ),
        name="expert_grads",
    )(me, got, grad_got, hid, grads)


def owner_kernel(count, me, *refs):
    arrived, outs = refs[:2], refs[2:]
    hidden = arrived[0].shape[2] // 3
    turn = pl.program_id(0)
    for place, values in enumerate(arrived):

        @pl.when(turn // count == me[0] ^ place)
        def _():
            full = values[0].astype(F32)
            outs[0][0] = full[:, :hidden]
            outs[1][0] = full[:, hidden : 2 * hidden]
            outs[2][0] = full[:, 2 * hidden :].T


def owner_grads(me, arrived):
    count, part, packed = arrived[0].shape
    hidden = packed // 3
    shape = jax.ShapeDtypeStruct
    one = lambda rows, cols: pl.BlockSpec((1, rows, cols), lambda e, me: (e, 0, 0))
    return pl.pallas_call(
        partial(owner_kernel, count),
        grid_spec=pltpu.PrefetchScalarGridSpec(
            num_scalar_prefetch=1,
            grid=(2 * count,),
            in_specs=[pl.BlockSpec((1, part, packed), lambda e, me: (e % count, 0, 0))] * 2,
            out_specs=[one(part, hidden), one(part, hidden), one(hidden, part)],
        ),
        out_shape=[shape((2 * count, part, hidden), F32)] * 2
        + [shape((2 * count, hidden, part), F32)],
        compiler_params=compiler_params(),
        cost_estimate=cost(0, 12 * count * part * packed),
        name="owner_grads",
    )(me, *arrived)


def combine_kernel(weighted, turned, *refs):
    if weighted:
        rows, places, table, number, gates, hidden, weight, out = refs
    else:
        rows, places, table, number, hidden, weight, out = refs
    experts, _, slots, width = rows.shape
    wide = low_dot(places[0], table[...])
    factor = low_dot(gates[0], table[...]) if weighted else 1.0
    chosen = jnp.where(wide == number[...], factor, 0.0).astype(BF16)
    total = low_dot(chosen, rows[:, 0].reshape(experts * slots, width))
    dense = dot_nt if turned else low_dot
    out[...] = (total + dense(hidden[...], weight[...])).astype(BF16)


def combine(rows, places, hidden, weight, turned, gates=None):
    experts, blocks, slots, width = rows.shape
    count = places.shape[1]
    expert_of = jnp.arange(experts * slots, dtype=jnp.int32) // slots
    table = (jnp.arange(experts, dtype=jnp.int32)[:, None] == expert_of[None, :]).astype(BF16)
    number = (jnp.arange(experts * slots, dtype=jnp.int32) % slots).astype(F32)[None, :]
    small = pl.BlockSpec((1, count, experts), lambda b: (b, 0, 0))
    arrays = [rows, places, table, number]
    specs = [
        pl.BlockSpec((experts, 1, slots, width), lambda b: (0, b, 0, 0)),
        small,
        pl.BlockSpec(table.shape, lambda b: (0, 0)),
        pl.BlockSpec(number.shape, lambda b: (0, 0)),
    ]
    if gates is not None:
        arrays.append(gates)
        specs.append(small)
    arrays += [hidden, weight]
    specs += [
        pl.BlockSpec((count, hidden.shape[1]), lambda b: (b, 0)),
        pl.BlockSpec(weight.shape, lambda b: (0, 0)),
    ]
    return pl.pallas_call(
        partial(combine_kernel, gates is not None, turned),
        grid=(blocks,),
        in_specs=specs,
        out_specs=pl.BlockSpec((count, width), lambda b: (b, 0)),
        out_shape=jax.ShapeDtypeStruct((blocks * count, width), BF16),
        compiler_params=compiler_params(),
        cost_estimate=cost(
            2 * blocks * count * width * (experts * slots + hidden.shape[1]),
            2 * blocks * experts * slots * width + 2 * blocks * count * width,
        ),
        name="combine",
    )(*arrays)


def swap(block, axis, stride):
    return lax.ppermute(
        block, axis, [(i, i ^ stride) for i in range(lax.axis_size(axis))]
    )


def bits(count):
    return [1 << i for i in range(count.bit_length() - 1)]


def bit_of(axis, stride):
    return (lax.axis_index(axis) // stride) % 2


def after(value, *earlier):
    return lax.optimization_barrier((value, earlier))[0]


def scatter_step(block, stride, left):
    left = list(reversed(bits(lax.axis_size(SEQ)))) if left is None else list(left)
    cols = block.shape[1]
    axis = left.index(stride)
    left.remove(stride)
    block = block.reshape((1 << axis, 2, -1, cols))
    place = bit_of(SEQ, stride)
    kept = lax.dynamic_index_in_dim(block, place, 1, False)
    sent = lax.dynamic_index_in_dim(block, 1 - place, 1, False)
    block = (kept.astype(F32) + swap(sent, SEQ, stride).astype(F32)).astype(block.dtype)
    return block.reshape(-1, cols), left


def sum_all(block, axis, strides):
    for stride in strides:
        block = block + swap(block, axis, stride)
    return block


def added(one, two):
    return (one.astype(F32) + two.astype(F32)).astype(BF16)


def gather_exp(block, strides):
    known = {0: block}
    for stride in strides:
        known.update({at | stride: swap(v, "exp", stride) for at, v in known.items()})
    for stride in strides:
        flipped = bit_of("exp", stride) == 1
        known = {at: jnp.where(flipped, known[at ^ stride], v) for at, v in known.items()}
    return jnp.concatenate([known[at] for at in range(len(known))], axis=0)


def scatter_exp(blocks, strides):
    place = lax.axis_index("exp")
    known = {
        at: lax.dynamic_index_in_dim(blocks, place ^ at, 0, False) for at in range(blocks.shape[0])
    }
    for stride in reversed(strides):
        known = {
            at: (v.astype(F32) + swap(known[at | stride], "exp", stride).astype(F32)).astype(
                F32 if len(known) == 2 else v.dtype
            )
            for at, v in known.items()
            if not at & stride
        }
    return known[0]


def split_rows(row):
    high = row.astype(BF16)
    rest = row - high.astype(F32)
    middle = rest.astype(BF16)
    return [high, middle, (rest - middle.astype(F32)).astype(BF16)]


def gather_states(through, state):
    rows = jnp.concatenate(split_rows(through), axis=0)
    packed = jnp.concatenate(
        [state.astype(BF16), jnp.pad(rows, ((0, 16 - rows.shape[0]), (0, 0)))], axis=0
    )
    gathered = lax.all_gather(packed, SEQ, axis=0).astype(F32)
    size = state.shape[0]
    return gathered[:, :size], jnp.sum(gathered[:, size : size + 3], axis=1, keepdims=True)


def earlier_states(states, decays):
    place = lax.axis_index(SEQ)
    total = jnp.zeros_like(states[0])
    for at in range(states.shape[0] - 1):
        total = jnp.where(at < place, states[at] + decays[at] * total, total)
    return total


def later_grads(grads, decays):
    place = lax.axis_index(SEQ)
    total = jnp.zeros_like(grads[0])
    for at in reversed(range(1, grads.shape[0])):
        total = jnp.where(at > place, grads[at] + decays[at] * total, total)
    return total


def per_device(
    tokens,
    segment_ids,
    routes,
    gate_weights,
    cotangent,
    norm_in,
    proj_z,
    proj_x,
    proj_bc,
    proj_dt,
    conv_weight,
    conv_bias,
    dt_bias,
    decay_log,
    skip_gain,
    gated_gain,
    proj_out,
    norm_mid,
    expert_gate,
    expert_up,
    expert_down,
    shared_gate,
    shared_up,
    shared_down,
):
    seq_pos = lax.axis_index(SEQ)
    exp_pos = lax.axis_index("exp")
    exp_count = lax.axis_size("exp")
    seq_count = lax.axis_size(SEQ)
    length, model_width = tokens.shape
    rows_here, top_count = routes.shape
    inner_width = gated_gain.shape[0]
    head_total = dt_bias.shape[0]
    pair_width = proj_bc.shape[1]
    state_dim = pair_width // 2
    local_width = proj_x.shape[1]
    head_count = proj_dt.shape[1]
    channels = local_width + pair_width
    col_start = exp_pos * local_width
    head_start = exp_pos * head_count
    low_z = seq_count // 4
    seq_strides = bits(seq_count)
    y_strides = bits(low_z)
    far_z = 2 * low_z
    exp_strides = list(reversed(bits(exp_count)))
    far_bit = bit_of(SEQ, far_z)
    block_count = 2 * exp_count
    span_count = length // SPAN

    pad_dt = jnp.pad(proj_dt, ((0, 0), (0, LANES - head_count)))
    projections = lax.all_gather(
        jnp.concatenate([proj_x, pad_dt, proj_z, proj_out.T], axis=1), SEQ, axis=0, tiled=True
    )
    weight_xdt = projections[:, : local_width + LANES]
    both = projections[:, local_width + LANES :]
    weight_x, weight_dt = weight_xdt[:, :local_width], weight_xdt[:, local_width:]
    halo_tokens = lax.ppermute(
        tokens[length - 8 :], SEQ, [(i, i + 1) for i in range(seq_count - 1)]
    )
    experts_here = expert_gate.shape[0]
    experts_half = experts_here // 2
    packed = jnp.concatenate(
        [expert_gate, expert_up, expert_down.transpose(0, 2, 1)], axis=2
    )
    kept = lax.dynamic_slice_in_dim(packed, far_bit * experts_half, experts_half, 0)
    sent = lax.dynamic_slice_in_dim(packed, (1 - far_bit) * experts_half, experts_half, 0)
    middle = experts_half // 2 if experts_half > 1 else experts_half
    low_0 = swap(kept, SEQ, 1)
    near_0 = swap(kept, SEQ, low_z)
    got_far = [swap(sent[:middle], SEQ, far_z)]

    hidden_part = shared_gate.shape[1] // block_count
    group_pos = far_bit * exp_count + exp_pos
    hidden_start = group_pos * hidden_part
    shared_in = jnp.concatenate(
        [
            lax.dynamic_slice_in_dim(shared_gate, hidden_start, hidden_part, 1),
            lax.dynamic_slice_in_dim(shared_up, hidden_start, hidden_part, 1),
        ],
        axis=1,
    )
    shared_back = lax.dynamic_slice_in_dim(shared_down, hidden_start, hidden_part, 0)

    tokens_f = tokens.astype(F32)
    scale_in = rms_scale(tokens_f)
    in_low = (tokens_f * scale_in * norm_in[None, :]).astype(BF16)
    halo_f = halo_tokens.astype(F32)
    halo_low = (halo_f * rms_scale(halo_f) * norm_in[None, :]).astype(BF16)
    raw_x = low_dot(in_low, weight_x)
    raw_s = low_dot(in_low, jnp.concatenate([proj_bc, weight_dt], axis=1))
    halo = jnp.concatenate([low_dot(halo_low, weight_x), low_dot(halo_low, proj_bc)], axis=1)
    padded_ids = jnp.concatenate([jnp.full((CONV - 1,), -1, jnp.int32), segment_ids])
    segs_ext = lax.dynamic_slice_in_dim(padded_ids, seq_pos * length, length + CONV - 1)
    segs = segs_ext[CONV - 1 :]
    spans = segs.reshape(span_count, SPAN)
    before = jnp.concatenate([segs_ext[CONV - 2 : CONV - 1], spans[:-1, -1]])
    marks = jnp.stack(
        [(segs_ext[tap : tap + length] == segs).astype(F32) for tap in range(CONV - 1)]
        + [
            (segs == segs_ext[CONV - 2]).astype(F32),
            (spans == before[:, None]).astype(F32).reshape(length),
            (spans == spans[:, -1:]).astype(F32).reshape(length),
            segs.astype(F32),
            jnp.zeros((length,), F32),
        ],
        axis=1,
    )
    seg_rows = segs.astype(F32).reshape(span_count, 1, SPAN)

    def local_cols(values):
        mine = lax.dynamic_slice_in_dim(values, col_start, local_width, values.ndim - 1)
        return jnp.concatenate([mine, values[..., inner_width:]], axis=-1)

    taps = jnp.concatenate(
        [
            local_cols(conv_weight),
            local_cols(conv_bias)[None, :],
            jnp.zeros((3, channels), F32),
        ],
        axis=0,
    )
    pad_heads = (0, LANES - head_count)
    dt_local = jnp.pad(lax.dynamic_slice_in_dim(dt_bias, head_start, head_count), pad_heads)
    rates_local = jnp.pad(
        -jnp.exp(lax.dynamic_slice_in_dim(decay_log, head_start, head_count)), pad_heads
    )
    lane_on = jnp.arange(LANES) < head_count
    raw_dt = raw_s[:, pair_width:] + dt_local[None, :]
    step_sizes = jnp.where(lane_on[None, :], jax.nn.softplus(raw_dt), 0.0)
    heads = jnp.concatenate(
        [dt_local[None, :], rates_local[None, :], jnp.zeros((6, LANES), F32)], axis=0
    )
    head_dim = local_width // head_count
    spread_f = (
        jnp.arange(LANES)[:, None] == (jnp.arange(local_width) // head_dim)[None, :]
    ).astype(F32)
    spread = spread_f.astype(BF16)

    raw_x, low_0, near_0, got_far[0] = lax.optimization_barrier(
        (raw_x, low_0, near_0, got_far[0])
    )
    if middle < experts_half:
        got_far.append(swap(after(sent[middle:], raw_x), SEQ, far_z))
    low_far = [swap(got_far[0], SEQ, 1)]
    route_cols = split_rows(gate_weights)
    route_cols = jnp.concatenate([routes.astype(BF16)] + route_cols, axis=1)
    route_cols = jnp.pad(route_cols, ((0, 0), (0, LANES - route_cols.shape[1])))
    cot_one = jnp.concatenate([cotangent, route_cols], axis=1)

    def tile(cols, turn=lambda i: i):
        return pl.BlockSpec((SPAN, cols), lambda i: (turn(i), 0))

    def whole(*shape):
        return pl.BlockSpec(shape, lambda i: (0,) * len(shape))

    def seg_tile(turn=lambda i: i):
        return pl.BlockSpec((1, 1, SPAN), lambda i: (turn(i), 0, 0))

    shape = jax.ShapeDtypeStruct
    elements = length * SPAN * head_count
    scan_cost = cost(
        4 * elements * LANES, length * (channels * 8 + local_width * 8 + 4096), elements
    )
    conv_out, inputs, bc_low, local_y, reach, entries, last_state = pl.pallas_call(
        scan_forward,
        grid=(span_count,),
        in_specs=[
            tile(local_width),
            tile(raw_s.shape[1]),
            whole(8, channels),
            tile(8),
            seg_tile(),
            whole(8, channels),
            tile(LANES),
            whole(8, LANES),
            whole(LANES, local_width),
        ],
        out_specs=[
            tile(channels),
            tile(local_width),
            tile(pair_width),
            tile(local_width),
            tile(LANES),
            pl.BlockSpec((1, state_dim, local_width), lambda i: (i, 0, 0)),
            whole(state_dim, local_width),
        ],
        out_shape=[
            shape((length, channels), F32),
            shape((length, local_width), BF16),
            shape((length, pair_width), BF16),
            shape((length, local_width), F32),
            shape((length, LANES), F32),
            shape((span_count, state_dim, local_width), F32),
            shape((state_dim, local_width), F32),
        ],
        scratch_shapes=[
            pltpu.VMEM((SPAN + 8, channels), F32),
            pltpu.VMEM((state_dim, local_width), F32),
            pltpu.VMEM((8, LANES), F32),
        ],
        compiler_params=compiler_params(),
        cost_estimate=scan_cost,
        name="scan_forward",
    )(raw_x, raw_s, halo, marks, seg_rows, taps, step_sizes, heads, spread)

    last_state, got_far, low_far[0] = lax.optimization_barrier(
        (last_state, got_far, low_far[0])
    )
    got_far = [after(part, last_state) for part in got_far]
    cot_far = swap(after(cot_one, last_state), SEQ, far_z)
    low_near = swap(after(near_0, last_state), SEQ, 1)
    low_far_rest = got_far[1:]
    got_far = jnp.concatenate(got_far, axis=0)
    near_far = swap(got_far, SEQ, low_z)
    through = jnp.dot(reach[length - 1 :], spread_f, precision=HIGH)
    block_states, block_decays = gather_states(through, last_state)
    state_in = earlier_states(block_states, block_decays)
    local_y, state_in, cot_far, near_far, low_near = lax.optimization_barrier(
        (local_y, state_in, cot_far, near_far, low_near)
    )
    low_far = low_far + [swap(after(part, local_y), SEQ, 1) for part in low_far_rest]
    weight_z, weight_out = both[:, :local_width], both[:, local_width:]
    gate_z = low_dot(in_low, weight_z)
    skip_wide = jnp.dot(
        jnp.pad(lax.dynamic_slice_in_dim(skip_gain, head_start, head_count), pad_heads)[None, :],
        spread_f,
        precision=HIGH,
    )
    gain_local = lax.dynamic_slice_in_dim(gated_gain, col_start, local_width)
    rows_wide = jnp.concatenate(
        [skip_wide, gain_local[None, :], jnp.zeros((6, local_width), F32)], axis=0
    )
    full_y, scaled_low, mixer_part, squares = pl.pallas_call(
        gate_forward,
        grid=(span_count,),
        in_specs=[
            tile(local_width),
            tile(LANES),
            tile(pair_width),
            whole(state_dim, local_width),
            tile(local_width),
            tile(local_width),
            whole(8, local_width),
            whole(LANES, local_width),
            whole(model_width, local_width),
        ],
        out_specs=[tile(local_width), tile(local_width), tile(model_width), tile(1)],
        out_shape=[
            shape((length, local_width), F32),
            shape((length, local_width), BF16),
            shape((length, model_width), BF16),
            shape((length, 1), F32),
        ],
        compiler_params=compiler_params(),
        cost_estimate=cost(
            2 * length * local_width * (model_width + 3 * LANES),
            length * (local_width * 16 + model_width * 2),
        ),
        name="gate_forward",
    )(local_y, reach, bc_low, state_in, inputs, gate_z, rows_wide, spread, weight_out)

    mixer_rows = scatter_exp(mixer_part.reshape(exp_count, rows_here, model_width), exp_strides)
    square_rows = scatter_exp(squares.reshape(exp_count, 1, rows_here), exp_strides)
    square_rows = square_rows.reshape(rows_here, 1)
    scale_mix = lax.rsqrt(square_rows / inner_width + EPS)
    residual = (
        lax.dynamic_slice_in_dim(tokens, exp_pos * rows_here, rows_here).astype(F32)
        + scale_mix * mixer_rows
    )
    scale_mid = rms_scale(residual)
    normed_mid = residual * scale_mid
    mid_low = (normed_mid * norm_mid[None, :]).astype(BF16)
    known = {0: after(cot_one, mixer_rows), exp_count: cot_far}
    for stride in exp_strides[:-1]:
        keys = list(known)
        far = swap(jnp.concatenate([known[at] for at in keys], axis=0), "exp", stride)
        for number, at in enumerate(keys):
            known[at | stride] = far[number * rows_here : (number + 1) * rows_here]
    mid_low, known, *low_far = lax.optimization_barrier((mid_low, known, *low_far))
    mid_all = lax.all_gather(mid_low, GROUP, axis=0, tiled=True)
    low_far_near = swap(near_far, SEQ, 1)
    low_far = jnp.concatenate(low_far, axis=0)
    keys = list(known)
    far = swap(jnp.concatenate([known[at] for at in keys], axis=0), "exp", 1)
    for number, at in enumerate(keys):
        known[at | 1] = far[number * rows_here : (number + 1) * rows_here]
    cot_all = jnp.concatenate([known[at] for at in range(block_count)], axis=0)

    def natural(values):
        return jnp.stack(
            [
                lax.dynamic_index_in_dim(values, at ^ group_pos, 0, False)
                for at in range(block_count)
            ]
        )

    capacity = 2 * rows_here * top_count // (experts_here * exp_count)
    first_expert = exp_pos * experts_here + far_bit * experts_half
    expert_ids = first_expert + jnp.arange(experts_half, dtype=jnp.int32)
    tables = cot_all[:, model_width:].reshape(block_count, rows_here, LANES)
    tables = natural(tables).astype(F32).transpose(0, 2, 1)
    routes_all = tables[:, :top_count].astype(jnp.int32)
    gates_all = sum(
        tables[:, at * top_count : (at + 1) * top_count] for at in range(1, 4)
    )
    named = routes_all[:, :, None, :] == expert_ids[None, None, :, None]
    hit = jnp.any(named, axis=1)
    gate_rows = jnp.sum(jnp.where(named, gates_all[:, :, None, :], 0.0), axis=1)
    order = jnp.triu(jnp.ones((rows_here, rows_here), BF16))
    rank = jnp.einsum("bes,st->bet", hit.astype(BF16), order, preferred_element_type=F32)
    places = jnp.where(hit, rank - 1.0, -1.0)
    place_rows = places.astype(jnp.int32)
    place_cols = places.transpose(0, 2, 1).astype(BF16)
    gate_cols = gate_rows.transpose(0, 2, 1).astype(BF16)
    group_here = jnp.reshape(group_pos, (1,)).astype(jnp.int32)
    grad_got = dispatch(
        cot_all, place_rows, capacity, model_width, gate_rows, group_here
    )
    cot_rows = cot_all[:, :model_width]
    grad_shid = dot_nt(cot_rows, shared_back).reshape(block_count, rows_here, hidden_part)
    grad_shid = natural(grad_shid).reshape(-1, hidden_part)
    sets = {
        0: kept,
        1: low_0,
        low_z: near_0,
        1 | low_z: low_near,
        far_z: got_far,
        1 | far_z: low_far,
        far_z | low_z: near_far,
        1 | far_z | low_z: low_far_near,
    }
    for stride in y_strides[1:]:
        sets.update({at | stride: swap(v, SEQ, stride) for at, v in sets.items()})
    mid_all, grad_got, grad_shid, *sets = lax.optimization_barrier(
        (mid_all, grad_got, grad_shid, *[sets[at] for at in range(seq_count)])
    )

    got = dispatch(mid_all, place_rows, capacity, model_width)
    place_here = jnp.reshape(seq_pos, (1,)).astype(jnp.int32)
    expert_hid, expert_back, expert_res, grad_rows = run_experts(place_here, got, grad_got, sets)
    shared_ab = low_dot(mid_all, shared_in)
    shared_a, shared_b = shared_ab[:, :hidden_part], shared_ab[:, hidden_part:]
    shared_hid = (jax.nn.silu(shared_a) * shared_b).astype(BF16)
    grad_ab = jnp.concatenate(
        [grad_shid * shared_b * silu_slope(shared_a), grad_shid * jax.nn.silu(shared_a)], axis=1
    ).astype(BF16)
    row_part = combine(grad_rows, place_cols, grad_ab, shared_in, True)
    grad_mid = lax.psum_scatter(row_part, GROUP, scatter_dimension=0, tiled=True)
    known = dict(
        enumerate(
            expert_grads(
                place_here, got, grad_got, after(expert_hid, row_part), expert_back, seq_count
            )
        )
    )

    def reduced(at, stride, *wait):
        sent = after(known[at | stride], *wait) if wait else known[at | stride]
        known[at] = added(known[at], swap(sent, SEQ, stride))
        return known[at]

    for stride in reversed(y_strides[1:]):
        for at in [at for at in known if at & stride]:
            reduced(at ^ stride, stride)
            del known[at]
    grad_ab = after(grad_ab, known[0])
    shared_grads = jnp.concatenate(
        [
            dot_tn(grad_ab, mid_all),
            dot_tn(
                natural(shared_hid.reshape(block_count, rows_here, -1)).reshape(
                    shared_hid.shape
                ),
                cot_rows,
            ),
        ],
        axis=0,
    ).astype(BF16)
    first_sum = reduced(low_z | far_z, 1)
    grad_mid, shared_grads = lax.optimization_barrier((grad_mid, shared_grads))
    grad_mid = grad_mid.astype(F32)
    second_sum = reduced(far_z, 1)
    shard = lax.psum_scatter(
        shared_grads, ("near", "low"), scatter_dimension=0, tiled=True
    )
    pieces = lax.all_gather(shard, ALL, axis=0, tiled=True)

    grad_norm_mid = jnp.sum(grad_mid * normed_mid, axis=0)
    grad_resid = cotangent.astype(F32) + norm_back(grad_mid, norm_mid, normed_mid, scale_mid)
    grad_part = (scale_mix * grad_resid).astype(BF16)
    grad_square = (
        jnp.sum(grad_resid * mixer_rows, axis=1, keepdims=True) * -0.5 * scale_mix**3 / inner_width
    ).astype(BF16)
    grad_part_all = gather_exp(grad_part, exp_strides)
    grad_square_all = gather_exp(grad_square.reshape(1, rows_here), exp_strides)
    grad_square_all = grad_square_all.astype(F32).reshape(length, 1)

    grad_part_all, known[far_z], known[low_z | far_z], expert_res = lax.optimization_barrier(
        (grad_part_all, known[far_z], known[low_z | far_z], expert_res)
    )
    out_part = combine(
        expert_res, place_cols, shared_hid, shared_back, False, gate_cols
    )
    third_sum = reduced(far_z, low_z)

    grad_y, grad_z, gate_sums, direct = pl.pallas_call(
        gate_backward,
        grid=(span_count,),
        in_specs=[
            tile(model_width),
            tile(1),
            tile(local_width),
            tile(local_width),
            tile(local_width),
            tile(LANES),
            tile(pair_width),
            whole(8, local_width),
            whole(LANES, local_width),
            whole(model_width, local_width),
        ],
        out_specs=[
            tile(local_width),
            tile(local_width),
            whole(8, local_width),
            whole(state_dim, local_width),
        ],
        out_shape=[
            shape((length, local_width), BF16),
            shape((length, local_width), BF16),
            shape((8, local_width), F32),
            shape((state_dim, local_width), F32),
        ],
        compiler_params=compiler_params(),
        cost_estimate=cost(
            2 * length * local_width * (model_width + 3 * LANES),
            length * (local_width * 16 + model_width * 2),
        ),
        name="gate_backward",
    )(
        grad_part_all,
        grad_square_all,
        full_y,
        gate_z,
        inputs,
        reach,
        bc_low,
        rows_wide,
        spread,
        weight_out,
    )
    fourth_sum = reduced(low_z, 1)
    state_grad = later_grads(
        lax.all_gather(direct.astype(BF16), SEQ, axis=0).astype(F32), block_decays
    )

    small_first = y_strides + [low_z, far_z]
    sent = jnp.concatenate([dot_tn(in_low, grad_z), dot_tn(grad_part_all, scaled_low)], axis=1)
    sent, third_sum, fourth_sum, known[1] = lax.optimization_barrier(
        (sent.astype(BF16), third_sum, fourth_sum, known[1])
    )
    far_back = [swap(third_sum[:middle], SEQ, far_z)]
    low_sent = swap(known[1], SEQ, 1)
    sent, sent_left = scatter_step(sent, small_first[0], None)
    grad_y, state_grad, out_part = lax.optimization_barrier((grad_y, state_grad, out_part))
    near_sent = swap(fourth_sum, SEQ, low_z)
    routed = lax.psum_scatter(out_part, GROUP, scatter_dimension=0, tiled=True).astype(F32)
    passed = jnp.concatenate([jnp.ones((1, LANES), F32), reach[SPAN - 1 : length - 1 : SPAN]])
    passed = jnp.broadcast_to(passed[:, None, :], (span_count, 8, LANES))
    turn = lambda i: span_count - 1 - i
    ahead = SPAN // 8
    before_tile = lambda cols: pl.BlockSpec(
        (8, cols), lambda i: (jnp.maximum(turn(i) * ahead - 1, 0), 0)
    )
    grad_x, grad_bc, grad_steps, tail_rows, head_rows, conv_sums, rate_sums = pl.pallas_call(
        scan_backward,
        grid=(span_count,),
        in_specs=[
            tile(channels, turn),
            tile(local_width, turn),
            tile(raw_s.shape[1], turn),
            before_tile(local_width),
            before_tile(raw_s.shape[1]),
            whole(8, channels),
            tile(8, turn),
            seg_tile(turn),
            whole(8, channels),
            tile(LANES, turn),
            whole(8, LANES),
            whole(LANES, local_width),
            whole(local_width, LANES),
            tile(local_width, turn),
            tile(pair_width, turn),
            tile(local_width, turn),
            tile(local_width, turn),
            pl.BlockSpec((1, state_dim, local_width), lambda i: (turn(i), 0, 0)),
            pl.BlockSpec((1, 8, LANES), lambda i: (turn(i), 0, 0)),
            whole(state_dim, local_width),
            whole(state_dim, local_width),
            whole(8, local_width),
        ],
        out_specs=[
            tile(local_width, turn),
            tile(pair_width, turn),
            tile(LANES, turn),
            whole(8, channels),
            whole(8, channels),
            whole(8, channels),
            whole(8, LANES),
        ],
        out_shape=[
            shape((length, local_width), BF16),
            shape((length, pair_width), BF16),
            shape((length, LANES), F32),
            shape((8, channels), F32),
            shape((8, channels), F32),
            shape((8, channels), F32),
            shape((8, LANES), F32),
        ],
        scratch_shapes=[pltpu.VMEM((SPAN + 8, channels), F32)] * 4
        + [pltpu.VMEM((state_dim, local_width), F32), pltpu.VMEM((local_width, SPAN), F32)],
        compiler_params=compiler_params(),
        cost_estimate=cost(
            10 * elements * LANES, length * (channels * 16 + local_width * 16 + 4096), elements
        ),
        name="scan_backward",
    )(
        conv_out,
        raw_x,
        raw_s,
        raw_x,
        raw_s,
        halo,
        marks,
        seg_rows,
        taps,
        step_sizes,
        heads,
        spread,
        spread.T,
        inputs,
        bc_low,
        full_y,
        grad_y,
        entries,
        passed,
        state_in,
        state_grad,
        rows_wide,
    )
    (
        grad_x,
        grad_bc,
        grad_steps,
        tail_rows,
        head_rows,
        conv_sums,
        rate_sums,
        far_back[0],
        third_sum,
        low_sent,
        near_sent,
        sent,
    ) = lax.optimization_barrier(
        (
            grad_x,
            grad_bc,
            grad_steps,
            tail_rows,
            head_rows,
            conv_sums,
            rate_sums,
            far_back[0],
            third_sum,
            low_sent,
            near_sent,
            sent,
        )
    )
    if middle < experts_half:
        far_back.append(swap(third_sum[middle:], SEQ, far_z))
    edge = jnp.stack(
        [
            sum(
                taps[tap] * marks[at - tap, tap] * head_rows[at - tap]
                for tap in range(at + 1)
            )
            for at in range(CONV - 1)
        ]
    )
    block_output = (residual + routed).astype(BF16)

    edge = jnp.pad(edge, ((8 - (CONV - 1), 0), (0, 0))).astype(BF16)
    edge_x, edge_bc = edge[:, :local_width], edge[:, local_width:]
    grad_dt_raw = grad_steps * jax.nn.sigmoid(raw_dt) * lane_on.astype(F32)[None, :]
    grad_dt = grad_dt_raw.astype(BF16)
    grad_late = jnp.concatenate(
        [
            dot_tn(in_low, grad_x) + dot_tn(halo_low, edge_x),
            dot_tn(in_low, grad_dt),
            dot_tn(in_low, grad_bc) + dot_tn(halo_low, edge_bc),
        ],
        axis=1,
    ).astype(BF16)
    grad_late, far_back = lax.optimization_barrier((grad_late, far_back))
    late_sum, late_left = scatter_step(grad_late, small_first[0], None)
    grad_x, late_sum = lax.optimization_barrier((grad_x, late_sum))
    for stride in small_first[1:]:
        sent, sent_left = scatter_step(sent, stride, sent_left)
    sent = sent.astype(F32)
    sum_wz, sum_wout = sent[:, :local_width], sent[:, local_width:].T
    last_sum = added(added(known[0], low_sent), near_sent)
    owned = owner_grads(
        jnp.reshape(far_bit, (1,)).astype(jnp.int32),
        [last_sum, jnp.concatenate(far_back, axis=0)],
    )
    grad_in = (
        dot_nt(grad_z, weight_z)
        + dot_nt(grad_x, weight_x)
        + dot_nt(grad_dt, weight_dt)
        + dot_nt(grad_bc, proj_bc)
    )
    for stride in small_first[1:]:
        late_sum, late_left = scatter_step(late_sum, stride, late_left)
        if stride == low_z:
            late_sum, owned = lax.optimization_barrier((late_sum, owned))
    sum_gate_e, sum_up_e, sum_down_e = owned
    late_sum, conv_sums, rate_sums, gate_sums, grad_norm_mid = lax.optimization_barrier(
        (late_sum, conv_sums, rate_sums, gate_sums, grad_norm_mid)
    )
    late_sum = late_sum.astype(F32)
    sum_wxdt = late_sum[:, : local_width + LANES]
    sum_wbc = sum_all(late_sum[:, local_width + LANES :], "exp", exp_strides).astype(BF16)
    for stride in seq_strides:
        other = swap(sum_wbc, SEQ, stride)
        low = bit_of(SEQ, stride) == 0
        sum_wbc = jnp.where(
            low,
            jnp.concatenate([sum_wbc, other], axis=0),
            jnp.concatenate([other, sum_wbc], axis=0),
        )
    normed_in = tokens_f * scale_in
    halo_scale = rms_scale(halo_f)
    halo_normed = halo_f * halo_scale
    edge_in = dot_nt(edge_x, weight_x) + dot_nt(edge_bc, proj_bc)
    grad_norm_in = jnp.sum(grad_in * normed_in, axis=0) + jnp.sum(edge_in * halo_normed, axis=0)
    edge_part = lax.ppermute(
        norm_back(edge_in, norm_in, halo_normed, halo_scale),
        SEQ,
        [(i + 1, i) for i in range(seq_count - 1)],
    )
    grad_in_part = norm_back(grad_in, norm_in, normed_in, scale_in).astype(BF16)
    grad_in_part = grad_in_part.at[length - 8 :].set(
        (grad_in_part[length - 8 :].astype(F32) + edge_part).astype(BF16)
    )
    tokens_grad = grad_resid + scatter_exp(
        grad_in_part.reshape(exp_count, rows_here, model_width), exp_strides
    )

    pieces = pieces.reshape(
        2, 2, low_z, exp_count, shard.shape[0], model_width
    ).transpose(0, 3, 1, 2, 4, 5)
    pieces = pieces.reshape(block_count, 3, hidden_part, model_width).transpose(1, 0, 2, 3)
    pieces = pieces.reshape(3, block_count * hidden_part, model_width)

    def rows_of(values):
        flat = values.reshape(-1)
        count = -(-flat.shape[0] // local_width)
        return jnp.pad(flat, (0, count * local_width - flat.shape[0])).reshape(count, local_width)

    skip_sums = jnp.dot(gate_sums[1:2], spread_f.T, precision=HIGH)
    head_rows3 = jnp.concatenate(
        [jnp.sum(grad_dt_raw, axis=0, keepdims=True), rate_sums[:1] * rates_local, skip_sums]
    )
    own_sums = jnp.concatenate(
        [
            conv_sums[: CONV + 1, :local_width],
            gate_sums[:1],
            jnp.pad(head_rows3, ((0, 0), (0, local_width - LANES))),
        ]
    )
    shared_sums = jnp.concatenate(
        [rows_of(conv_sums[: CONV + 1, local_width:]), rows_of(grad_norm_mid)]
    )
    own_count = own_sums.shape[0]
    all_sums = sum_all(jnp.concatenate([own_sums, shared_sums]), SEQ, seq_strides)
    shared_sums = sum_all(all_sums[own_count:], "exp", exp_strides).reshape(-1)
    own_all = gather_exp(all_sums[None, :own_count], exp_strides)
    sum_norm_in = sum_all(
        sum_all(rows_of(grad_norm_in), SEQ, seq_strides), "exp", exp_strides
    ).reshape(-1)[:model_width]
    wide = own_all.transpose(1, 0, 2).reshape(own_count, inner_width)
    head_sums = own_all[:, CONV + 2 :, :head_count].transpose(1, 0, 2).reshape(3, head_total)
    pair_count = (CONV + 1) * pair_width
    pair_sums = shared_sums[:pair_count].reshape(CONV + 1, pair_width)
    pair_rows = -(-pair_count // local_width) * local_width
    conv_all = jnp.concatenate([wide[: CONV + 1], pair_sums], axis=1)
    return (
        block_output,
        tokens_grad,
        sum_norm_in,
        sum_wz,
        sum_wxdt[:, :local_width],
        sum_wbc.astype(F32),
        sum_wxdt[:, local_width : local_width + head_count],
        conv_all[:CONV],
        conv_all[CONV],
        head_sums[0],
        head_sums[1],
        head_sums[2],
        wide[CONV + 1],
        sum_wout,
        shared_sums[pair_rows : pair_rows + model_width],
        sum_gate_e,
        sum_up_e,
        sum_down_e,
        pieces[0].T.astype(F32),
        pieces[1].T.astype(F32),
        pieces[2].astype(F32),
    )


def solution(mesh):
    placed = (
        P(SEQ, None),
        P(),
        P(ALL, None),
        P(ALL, None),
        P(ALL, None),
        P(),
        P(SEQ, "exp"),
        P(SEQ, "exp"),
        P(),
        P(SEQ, "exp"),
        P(),
        P(),
        P(),
        P(),
        P(),
        P(),
        P("exp", SEQ),
        P(),
        P("exp", SEQ, None),
        P("exp", SEQ, None),
        P("exp", None, SEQ),
        P(),
        P(),
        P(),
    )
    seq_count, exp_count = mesh.devices.shape
    split = Mesh(
        mesh.devices.reshape(2, 2, seq_count // 4, exp_count), ("far", "near", "low", "exp")
    )
    return jax.shard_map(
        per_device,
        mesh=split,
        in_specs=placed,
        out_specs=(
            P(ALL, None),
            P(ALL, None),
            P(),
            P(SEQ, "exp"),
            P(SEQ, "exp"),
            P(),
            P(SEQ, "exp"),
            P(),
            P(),
            P(),
            P(),
            P(),
            P(),
            P("exp", SEQ),
            P(),
            P("exp", SEQ, None),
            P("exp", SEQ, None),
            P("exp", None, SEQ),
            P(),
            P(),
            P(),
        ),
        check_vma=False,
    )
```
